1024 devices in a mesh: patch: 128 (over z, x, core), elem: 8 (over y).
Axes of the slice: x: 4, y: 8, z: 16, core: 2. Of those that a mesh axis runs over, the one named last changes fastest.
Arguments:
- positions: float32 [3, 262144], P(None, ('patch', 'elem')), may hold values from -6 to 6
- target: float32 [3, 262144], P(None, ('patch', 'elem')), may hold values from -6 to 6
- inertia: float32 [1, 262144], P(None, ('patch', 'elem')), may hold values from 1 to 10
- incidence: int32 [3, 786432], P(None, ('patch', 'elem')), may hold values from 0 to 2047
- rest_inverse: float32 [4, 786432], P(None, ('patch', 'elem')), may hold values from -4 to 4
- counts: int32 [1024], P(('patch', 'elem')), may hold values from 192 to 768
- w_in: bfloat16 [128, 6], replicated, may hold values from -2.5 to 2.5
- w_hid1: bfloat16 [128, 128], replicated, may hold values from -0.5 to 0.5
- w_hid2: bfloat16 [128, 128], replicated, may hold values from -0.5 to 0.5
- w_out: bfloat16 [90, 128], replicated, may hold values from -0.5 to 0.5
Outputs:
- solution_field: float32 [3, 262144], P(None, ('patch', 'elem'))
- residual: float32 [3, 262144], P(None, ('patch', 'elem'))
The draws below stay inside these ranges and needn't reach their ends.
All inputs are finite; a program needn't handle non-finite values.
Results may differ from the reference program's by a relative error of at most 0.0055.
Values sent between devices are 32-bit elements; how exact they have to be, the bound alone decides.
No kernel may reach another device: no remote copies, remote signals or barrier semaphores. Data moves between devices by JAX's collectives and lax.ppermute only.
A program may use at most 32 MiB of HBM per device.

```python
import math
import jax
import jax.numpy as jnp
from jax import lax

HIDDEN_SIZE = 128
TRI_DEV = 768
ITERS = 3
PATCH_VERTS = 2048
PATCH_TRIS = 6144
TRIS = 786432
VERTS = 262144
DEVICES = 1024


def touch_ends(array, key, low, top_value):
    longest = array.shape.index(max(array.shape))
    spots = []
    for shift in (0, 1):
        where = [jax.random.randint(jax.random.fold_in(key, axis), (), 0, length) for axis, length in enumerate(array.shape)]
        where[longest] = (where[longest] + shift) % array.shape[longest]
        spots.append(tuple(where))
    return array.at[spots[0]].set(low).at[spots[1]].set(top_value)


def shard_levels(stream_key, dims, cuts, least, largest):
    gain, own = 1.0, jax.random.fold_in(stream_key, 6)
    for dim, parts in cuts:
        heights = jnp.exp(jax.random.uniform(jax.random.fold_in(own, dim), (parts,), jnp.float32, least / len(cuts), largest / len(cuts)))
        gain = gain * jnp.repeat(heights, dims[dim] // parts).reshape([-1 if axis == dim else 1 for axis in range(len(dims))])
    return gain


def centred(own_key, dims, spread, reach, cuts=(), kind=jnp.bfloat16):
    drawn = jax.random.normal(own_key, dims, jnp.float32) * spread
    if len(cuts) > 0:
        drawn = shard_levels(own_key, dims, cuts, -0.22, 0.18) * drawn
    return jnp.clip(drawn, min=-reach, max=reach).astype(kind)


def setup_inputs(seed: int = 0) -> dict:
    seeds = jax.random.split(jax.random.key(seed), 11)
    return {
        "positions": centred(seeds[0], (3, VERTS), 1.0, 6.0, ((1, 1024),), jnp.float32),
        "target": centred(seeds[1], (3, VERTS), 1.0, 6.0, ((1, 1024),), jnp.float32),
        "inertia": jnp.clip(jnp.exp(math.log(10.0) - 2.3025851 * jax.random.uniform(seeds[2], (1, VERTS), jnp.float32) ** shard_levels(seeds[2], (1, VERTS), ((1, 1024),), -0.2, 0.2)), 1.0, 10.0),
        "incidence": touch_ends(jax.random.randint(seeds[3], (3, TRIS), 0, PATCH_VERTS), jax.random.fold_in(seeds[3], 1), 0, PATCH_VERTS - 1).astype(jnp.int32),
        "rest_inverse": centred(seeds[4], (4, TRIS), 0.7, 4.0, ((1, 1024),), jnp.float32),
        "counts": touch_ends(jax.random.randint(seeds[5], (DEVICES,), TRI_DEV // 4, TRI_DEV + 1), jax.random.fold_in(seeds[5], 1), TRI_DEV // 4, TRI_DEV).astype(jnp.int32),
        "w_in": centred(seeds[6], (HIDDEN_SIZE, 6), 6 ** -0.5, 2.5),
        "w_hid1": centred(seeds[7], (HIDDEN_SIZE, HIDDEN_SIZE), HIDDEN_SIZE ** -0.5, 0.5),
        "w_hid2": centred(seeds[8], (HIDDEN_SIZE, HIDDEN_SIZE), HIDDEN_SIZE ** -0.5, 0.5),
        "w_out": centred(seeds[9], (90, HIDDEN_SIZE), HIDDEN_SIZE ** -0.5, 0.5),
    }


STIFF = 1.0
REG = 0.1


def triangle_terms(pos, inc, rinv, valid, w_in, w_hid1, w_hid2, w_out):
    corner = [pos[:, inc[k]] for k in range(3)]
    edge_one = corner[1] - corner[0]
    edge_two = corner[2] - corner[0]
    feats = jnp.concatenate([edge_one * rinv[0] + edge_two * rinv[2], edge_one * rinv[1] + edge_two * rinv[3]], axis=0).astype(jnp.bfloat16)
    hidden = jnp.tanh(jnp.dot(w_in, feats, preferred_element_type=jnp.float32)).astype(jnp.bfloat16)
    hidden = jnp.tanh(jnp.dot(w_hid1, hidden, preferred_element_type=jnp.float32)).astype(jnp.bfloat16)
    hidden = jnp.tanh(jnp.dot(w_hid2, hidden, preferred_element_type=jnp.float32)).astype(jnp.bfloat16)
    output = jnp.dot(w_out, hidden, preferred_element_type=jnp.float32)
    stress = output[:9] * valid
    factor = (output[9:] * valid).astype(jnp.bfloat16)
    return stress, factor


def scatter_rows(values, inc, count):
    accum = jnp.zeros((3, count), jnp.float32)
    for k in range(3):
        accum = accum.at[:, inc[k]].add(values[3 * k:3 * k + 3])
    return accum


def hess_diag(factor, valid):
    full = factor.astype(jnp.float32).reshape(9, 9, -1)
    return jnp.sum(full * full, axis=1) / 9.0 + REG * valid


def tri_apply(vec, inc, factor, valid, count):
    gathered = jnp.concatenate([vec[:, inc[k]] for k in range(3)], axis=0)
    full = factor.astype(jnp.float32).reshape(9, 9, -1)
    inner = jnp.sum(full * gathered[:, None, :], axis=0)
    result = jnp.sum(full * inner[None, :, :], axis=1) / 9.0 + REG * valid * gathered
    return scatter_rows(result, inc, count)


def chain(vec):
    padded = jnp.pad(vec, ((0, 0), (1, 1)))
    return STIFF * (2.0 * vec - padded[:, :-2] - padded[:, 2:])


def reference(positions, target, inertia, incidence, rest_inverse, counts, w_in, w_hid1, w_hid2, w_out):
    npatch = VERTS // PATCH_VERTS
    groups = PATCH_TRIS // TRI_DEV

    def patchify(arr):
        return arr.reshape(arr.shape[0], npatch, -1).transpose(1, 0, 2)

    def unpatch(arr):
        return arr.transpose(1, 0, 2).reshape(arr.shape[1], -1)

    inc_p = patchify(incidence)
    rin_p = patchify(rest_inverse)
    cnt_p = counts.reshape(npatch, groups)
    slots = jnp.arange(PATCH_TRIS, dtype=jnp.int32)
    slot_in = slots % TRI_DEV
    group_of = slots // TRI_DEV

    def valid_of(cnt):
        return (slot_in < cnt[group_of]).astype(jnp.float32)

    def setup(item):
        pos, inc, rin, cnt = item
        valid = valid_of(cnt)
        stress, factor = triangle_terms(pos, inc, rin, valid, w_in, w_hid1, w_hid2, w_out)
        return scatter_rows(stress, inc, PATCH_VERTS), scatter_rows(hess_diag(factor, valid), inc, PATCH_VERTS), factor

    grad_tri, diag_tri, factors = lax.map(setup, (patchify(positions), inc_p, rin_p, cnt_p))
    gradient = inertia * (positions - target) + unpatch(grad_tri) + chain(positions)
    diagonal = inertia + unpatch(diag_tri) + 2.0 * STIFF

    def operate(vec):
        def one(item):
            piece, inc, factor, cnt = item
            return tri_apply(piece, inc, factor, valid_of(cnt), PATCH_VERTS)
        tri = lax.map(one, (patchify(vec), inc_p, factors, cnt_p))
        return inertia * vec + unpatch(tri) + chain(vec)

    solution_field = jnp.zeros_like(positions)
    residual = -gradient
    precond = residual / diagonal
    direction = precond
    rz_now = jnp.sum(residual * precond)
    for step in range(ITERS):
        image = operate(direction)
        alpha = rz_now / jnp.sum(direction * image)
        solution_field = solution_field + alpha * direction
        residual = residual - alpha * image
        if step + 1 < ITERS:
            precond = residual / diagonal
            rz_next = jnp.sum(residual * precond)
            direction = precond + (rz_next / rz_now) * direction
            rz_now = rz_next
    return solution_field, residual
```

```python
import functools

import jax
import jax.numpy as jnp
from jax import lax
from jax.experimental import pallas as pl
from jax.experimental.pallas import tpu as pltpu
from jax.sharding import PartitionSpec as P

STIFF = 1.0
REG = 0.1
GROUPS = 8
LANES = 128
TRI_CHUNKS = 6
VERT_CHUNKS = 2
ROWS = VERT_CHUNKS * GROUPS
TRI_ROWS = TRI_CHUNKS * GROUPS

POS, TGT, INERTIA, COUNT, INC, RINV, RIM, PACKED = 0, 6, 12, 14, 16, 34, 58, 64

F32 = jnp.float32
BF16 = jnp.bfloat16


def vmem(n):
    return [pl.BlockSpec(memory_space=pltpu.VMEM)] * n


def iota(shape, axis):
    return lax.broadcasted_iota(jnp.int32, shape, axis)


def pack_kernel(pos, tgt, inertia, inc, rinv, counts, rim, out):
    first = lax.axis_index("elem") == 0
    out[0] = jnp.zeros((PACKED, LANES), F32)
    for k in range(VERT_CHUNKS):
        cut = slice(k * LANES, (k + 1) * LANES)
        out[0, POS + 3 * k : POS + 3 * k + 3] = pos[:, cut]
        out[0, TGT + 3 * k : TGT + 3 * k + 3] = tgt[:, cut]
        out[0, INERTIA + k : INERTIA + k + 1] = inertia[:, cut]
    out[0, COUNT : COUNT + 1] = jnp.full((1, LANES), counts[0], jnp.int32).astype(F32)
    for k in range(TRI_CHUNKS):
        cut = slice(k * LANES, (k + 1) * LANES)
        out[0, INC + 3 * k : INC + 3 * k + 3] = inc[:, cut].astype(F32)
        out[0, RINV + 4 * k : RINV + 4 * k + 4] = rinv[:, cut]
    out[0, RIM : RIM + 3] = jnp.where(first, rim[:, LANES:], rim[:, :LANES])
    block = out[0]
    for e in range(1, GROUPS):
        out[e] = block


def lane_rows(ref, row):
    return ref[pl.ds(row, GROUPS, stride=PACKED), :]


def corner_of(whole, k, q):
    index = lane_rows(whole, INC + 3 * k + q).astype(jnp.int32)
    row = ((index >> 7) & 1) * GROUPS + (index >> 8)
    return row, index & (LANES - 1)


def valid_of(whole, k):
    slot = iota((GROUPS, LANES), 1) + k * LANES
    return (slot.astype(F32) < lane_rows(whole, COUNT)).astype(F32)


def gather(field, row, lane):
    found = [jnp.zeros((GROUPS, LANES), F32)] * 3
    for h in range(ROWS):
        here = row == h
        for c in range(3):
            line = jnp.broadcast_to(field[c * ROWS + h : c * ROWS + h + 1, :], (GROUPS, LANES))
            value = jnp.take_along_axis(line, lane, axis=1, mode="promise_in_bounds")
            found[c] = jnp.where(here, value, found[c])
    return found


def scatter(values, row, lane, stage):
    comps = len(values)
    stage[0:8] = row.astype(F32)
    stage[8:16] = lane.astype(F32)
    for c, value in enumerate(values):
        upper = value.astype(BF16).astype(F32)
        stage[16 + 8 * c : 24 + 8 * c] = upper
        stage[16 + 8 * (comps + c) : 24 + 8 * (comps + c)] = value - upper
    rows_of = iota((ROWS, LANES), 0).astype(F32)
    lanes_of = iota((LANES, LANES), 0).astype(F32)
    left, right = [], []
    for e in range(GROUPS):
        def line(at, count):
            return jnp.broadcast_to(stage[at + e : at + e + 1, :], (count, LANES))
        here = line(0, ROWS) == rows_of
        left.append(jnp.concatenate(
            [jnp.where(here, line(16 + 8 * c, ROWS), 0.0).astype(BF16) for c in range(2 * comps)], axis=0))
        right.append(jnp.where(line(8, LANES) == lanes_of, 1.0, 0.0).astype(BF16))
    return lax.dot_general(
        jnp.concatenate(left, axis=1), jnp.concatenate(right, axis=1),
        (((1,), (1,)), ((), ())), preferred_element_type=F32)


def chain(here, before=None, after=None):
    lane = iota((GROUPS, LANES), 1)
    sub = iota((GROUPS, LANES), 0)
    low, high = here
    low_up, high_up = pltpu.roll(low, 1, 1), pltpu.roll(high, 1, 1)
    low_down, high_down = pltpu.roll(low, LANES - 1, 1), pltpu.roll(high, LANES - 1, 1)
    edge = 0.0 if before is None else pltpu.roll(jnp.broadcast_to(before, (GROUPS, LANES)), 1, 1)
    rim = jnp.where(sub == 0, edge, pltpu.roll(high_up, 1, 0))
    before_low = jnp.where(lane == 0, rim, low_up)
    before_high = jnp.where(lane == 0, low_up, high_up)
    edge = 0.0 if after is None else pltpu.roll(jnp.broadcast_to(after, (GROUPS, LANES)), LANES - 1, 1)
    rim = jnp.where(sub == GROUPS - 1, edge, pltpu.roll(low_down, GROUPS - 1, 0))
    after_low = jnp.where(lane == LANES - 1, high_down, low_down)
    after_high = jnp.where(lane == LANES - 1, rim, high_down)
    return (STIFF * (2.0 * low - before_low - after_low), STIFF * (2.0 * high - before_high - after_high))


def chunks(ref, c):
    at = c * ROWS
    return ref[at : at + GROUPS, :], ref[at + GROUPS : at + ROWS, :]


def put(ref, c, pair):
    at = c * ROWS
    ref[at : at + GROUPS, :] = pair[0]
    ref[at + GROUPS : at + ROWS, :] = pair[1]


def elements(whole, factors, field, stage, total):
    total[0 : 6 * ROWS] = jnp.zeros((6 * ROWS, LANES), F32)

    @pl.loop(0, TRI_CHUNKS)
    def _(k):
        places = [corner_of(whole, k, q) for q in range(3)]
        u = []
        for row, lane in places:
            u += gather(field, row, lane)

        def factor(j, m):
            return factors[pl.ds(pl.multiple_of((9 * j + m) * TRI_ROWS + k * GROUPS, GROUPS), GROUPS), :]

        inner = [sum(factor(j, m) * u[j] for j in range(9)) * (1.0 / 9.0) for m in range(9)]
        shift = REG * valid_of(whole, k)
        out = [sum(factor(j, m) * inner[m] for m in range(9)) + shift * u[j] for j in range(9)]
        part = 0.0
        for q, (row, lane) in enumerate(places):
            part += scatter(out[3 * q : 3 * q + 3], row, lane, stage)
        total[0 : 6 * ROWS] += part

    total[0 : 3 * ROWS] = total[0 : 3 * ROWS] + total[3 * ROWS : 6 * ROWS]


def inertia_of(whole):
    return [lane_rows(whole, INERTIA + k) for k in range(VERT_CHUNKS)]


def apply_local(whole, factors, field, stage, total, befores=None, afters=None):
    elements(whole, factors, field, stage, total)
    mass = inertia_of(whole)
    out = []
    for c in range(3):
        v = chunks(field, c)
        bent = chain(v, befores and befores[c], afters and afters[c])
        felt = chunks(total, c)
        out.append([mass[k] * v[k] + bent[k] + felt[k] for k in range(VERT_CHUNKS)])
    return out


def setup_kernel(whole, w_in, w_hid1, w_hid2, w_out, factors, first, image, diagonal, up, down,
                 pos, feats, w_first, w_last, raw, stage, total):
    for c in range(3):
        put(pos, c, [lane_rows(whole, POS + 3 * k + c) for k in range(VERT_CHUNKS)])
    feats[...] = jnp.zeros_like(feats)
    w_first[...] = jnp.zeros_like(w_first)
    w_first[:, 0:6] = w_in[...].astype(F32)
    w_last[...] = jnp.zeros_like(w_last)
    w_last[0:90, :] = w_out[...].astype(F32)
    w1 = w_first[...].astype(BF16)
    w4 = w_last[...].astype(BF16)
    total[...] = jnp.zeros_like(total)

    @pl.loop(0, TRI_CHUNKS)
    def _(k):
        places = [corner_of(whole, k, q) for q in range(3)]
        x0, x1, x2 = [gather(pos, row, lane) for row, lane in places]
        a, b, c_, d = [lane_rows(whole, RINV + 4 * k + i) for i in range(4)]
        for c in range(3):
            one, two = x1[c] - x0[c], x2[c] - x0[c]
            feats[pl.ds(c, GROUPS, stride=16), :] = one * a + two * c_
            feats[pl.ds(3 + c, GROUPS, stride=16), :] = one * b + two * d
        x = jnp.concatenate([feats[16 * e : 16 * e + 16, :] for e in range(GROUPS)], axis=1).astype(BF16)
        h = jnp.tanh(jnp.dot(w1, x, preferred_element_type=F32)).astype(BF16)
        h = jnp.tanh(jnp.dot(w_hid1[...], h, preferred_element_type=F32)).astype(BF16)
        h = jnp.tanh(jnp.dot(w_hid2[...], h, preferred_element_type=F32)).astype(BF16)
        o = jnp.dot(w4, h, preferred_element_type=F32)
        for e in range(GROUPS):
            for g in range(12):
                raw[pl.ds(g * 64 + e, 8, stride=8), :] = o[8 * g : 8 * g + 8, e * LANES : (e + 1) * LANES]
        valid = valid_of(whole, k)
        forces, curves = [], []
        for j in range(9):
            forces.append(raw[8 * j : 8 * j + 8, :] * valid)
            curve = 0.0
            for m in range(9):
                at = 9 * j + m
                g = (raw[8 * (9 + at) : 8 * (9 + at) + 8, :] * valid).astype(BF16).astype(F32)
                factors[pl.ds(pl.multiple_of(at * TRI_ROWS + k * GROUPS, GROUPS), GROUPS), :] = g
                curve += g * g
            curves.append(curve * (1.0 / 9.0) + REG * valid)
        part = 0.0
        for q, (row, lane) in enumerate(places):
            part += scatter(forces[3 * q : 3 * q + 3] + curves[3 * q : 3 * q + 3], row, lane, stage)
        total[...] += part

    total[0 : 6 * ROWS] = total[0 : 6 * ROWS] + total[6 * ROWS : 12 * ROWS]
    mass = inertia_of(whole)
    inverse = []
    for c in range(3):
        x = chunks(pos, c)
        bent = chain(x, whole[RIM + c : RIM + c + 1, :],
                     whole[(GROUPS - 1) * PACKED + RIM + c : (GROUPS - 1) * PACKED + RIM + c + 1, :])
        felt, curve = chunks(total, c), chunks(total, 3 + c)
        diag = [mass[k] + curve[k] + 2.0 * STIFF for k in range(VERT_CHUNKS)]
        inv = [1.0 / diag[k] for k in range(VERT_CHUNKS)]
        grad = [mass[k] * (x[k] - lane_rows(whole, TGT + 3 * k + c)) + bent[k] + felt[k]
                for k in range(VERT_CHUNKS)]
        put(diagonal, c, diag)
        put(first, c, [-grad[k] * inv[k] for k in range(VERT_CHUNKS)])
        inverse.append(inv)
    w = apply_local(whole, factors, first, stage, total)
    up[...] = jnp.zeros_like(up)
    down[...] = jnp.zeros_like(down)
    for c in range(3):
        v = chunks(first, c)
        put(image, c, w[c])
        nxt = [w[c][k] * inverse[c][k] - v[k] for k in range(VERT_CHUNKS)]
        for i, what in enumerate((v, nxt, inverse[c])):
            up[3 * i + c : 3 * i + c + 1, :] = what[1][GROUPS - 1 : GROUPS, :]
            down[3 * i + c : 3 * i + c + 1, :] = what[0][0:1, :]


def krylov_kernel(whole, factors, first, image, diagonal, above, below,
                  second, third, last_image, sums, stage, total):
    lane = iota((GROUPS, LANES), 1)
    sub = iota((GROUPS, LANES), 0)
    head = (lane == 0) & (sub == 0)
    tail = (lane == LANES - 1) & (sub == GROUPS - 1)

    def spread(row):
        return jnp.broadcast_to(row, (GROUPS, LANES))

    befores, afters = [], []
    for c in range(3):
        v0, w0 = chunks(first, c), chunks(image, c)
        diag = chunks(diagonal, c)
        inv = [1.0 / diag[k] for k in range(VERT_CHUNKS)]
        old_up, old_down = above[c : c + 1, :], below[c : c + 1, :]
        w_low = w0[0] - STIFF * jnp.where(head, pltpu.roll(spread(old_up), 1, 1), 0.0)
        w_high = w0[1] - STIFF * jnp.where(tail, pltpu.roll(spread(old_down), LANES - 1, 1), 0.0)
        put(second, c, [w_low * inv[0] - v0[0], w_high * inv[1] - v0[1]])
        mine_low = pltpu.roll(spread(v0[0][0:1, :]), LANES - 1, 1)[0:1, :]
        mine_high = pltpu.roll(spread(v0[1][GROUPS - 1 : GROUPS, :]), 1, 1)[0:1, :]
        befores.append(above[3 + c : 4 + c, :] - STIFF * mine_low * above[6 + c : 7 + c, :])
        afters.append(below[3 + c : 4 + c, :] - STIFF * mine_high * below[6 + c : 7 + c, :])
    w = apply_local(whole, factors, second, stage, total, befores, afters)
    for c in range(3):
        diag, v1 = chunks(diagonal, c), chunks(second, c)
        put(third, c, [w[c][k] / diag[k] - v1[k] for k in range(VERT_CHUNKS)])
    w = apply_local(whole, factors, third, stage, total)
    moment = [0.0] * 6
    ends = []
    for c in range(3):
        put(last_image, c, w[c])
        diag = chunks(diagonal, c)
        v0, v1, v2 = chunks(first, c), chunks(second, c), chunks(third, c)
        for k in range(VERT_CHUNKS):
            m0, m1, m2 = diag[k] * v0[k], diag[k] * v1[k], diag[k] * v2[k]
            for i, term in enumerate((m0 * v0[k], m0 * v1[k], m1 * v1[k], m1 * v2[k], m2 * v2[k],
                                      v2[k] * w[c][k] - m2 * v2[k])):
                moment[i] += term
        ends.append((jnp.where(head, v2[0], 0.0), jnp.where(tail, v2[1], 0.0)))
    line = jnp.zeros((1, LANES), F32)
    for i, part in enumerate(moment + [x[0] for x in ends] + [x[1] for x in ends]):
        value = jnp.sum(jnp.sum(part, axis=0, keepdims=True), axis=1, keepdims=True)
        line = jnp.where(iota((1, LANES), 1) == i, value, line)
    sums[...] = jnp.broadcast_to(line, sums.shape)


def finish_kernel(sums, first, second, third, last_image, diagonal, field, residual):
    patch, elem = lax.axis_index("patch"), lax.axis_index("elem")
    patches = sums.shape[0]
    every = sums[...]
    lane = iota(every.shape, 1)
    sub = iota(every.shape, 0)
    totals = jnp.sum(every, axis=0, keepdims=True)

    def pick(row, i):
        return jnp.sum(jnp.where(iota((1, LANES), 1) == i, row, 0.0), axis=1, keepdims=True)

    after = pltpu.roll(pltpu.roll(every, patches - 1, 0), 3, 1)
    coupled = jnp.where((lane >= 9) & (lane < 12) & (sub < patches - 1), every * after, 0.0)
    coupling = jnp.sum(jnp.sum(coupled, axis=0, keepdims=True), axis=1, keepdims=True)
    mu = [pick(totals, i) for i in range(6)]
    mu[5] = mu[5] - 2.0 * STIFF * coupling

    def inner(p, q):
        return sum(a * b * mu[i + j] for i, a in enumerate(p) for j, b in enumerate(q))

    def applied(p):
        padded = list(p) + [0.0 * mu[0]]
        return [padded[0]] + [padded[j] + padded[j - 1] for j in range(1, len(padded))]

    one = jnp.ones((1, 1), F32)
    z, direction, x = [one], [one], []
    rz = inner(z, z)
    for step in range(3):
        ahead = applied(direction)
        alpha = rz / inner(direction, ahead)
        x = [(x[j] if j < len(x) else 0.0) + alpha * direction[j] for j in range(len(direction))]
        z = [(z[j] if j < len(z) else 0.0) - alpha * ahead[j] for j in range(len(ahead))]
        if step < 2:
            new = inner(z, z)
            ratio = new / rz
            direction = [z[j] + (ratio * direction[j] if j < len(direction) else 0.0) for j in range(len(z))]
            rz = new
    place = iota((1, LANES), 1)
    prev = sums[pl.ds(jnp.maximum(patch - 1, 0), 1), :]
    nxt = sums[pl.ds(jnp.minimum(patch + 1, patches - 1), 1), :]
    at_head = (place == 0) & (elem == 0) & (patch > 0)
    at_tail = (place == LANES - 1) & (elem == GROUPS - 1) & (patch < patches - 1)
    for c in range(3):
        for k in range(VERT_CHUNKS):
            at = pl.ds(c * ROWS + k * GROUPS + elem, 1)
            v0, v1, v2, w2, diag = first[at, :], second[at, :], third[at, :], last_image[at, :], diagonal[at, :]
            if k == 0:
                w2 = w2 - STIFF * jnp.where(at_head, pick(prev, 9 + c), 0.0)
            else:
                w2 = w2 - STIFF * jnp.where(at_tail, pick(nxt, 6 + c), 0.0)
            v3 = w2 / diag - v2
            cut = slice(k * LANES, (k + 1) * LANES)
            field[c : c + 1, cut] = x[0] * v0 + x[1] * v1 + x[2] * v2
            residual[c : c + 1, cut] = diag * (z[0] * v0 + z[1] * v1 + z[2] * v2 + z[3] * v3)


def shape(*dims):
    return jax.ShapeDtypeStruct(dims, F32)


def per_device(positions, target, inertia, incidence, rest_inverse, counts, w_in, w_hid1, w_hid2, w_out):
    patches = lax.axis_size("patch")
    params = pltpu.CompilerParams(vmem_limit_bytes=48 * 1024 * 1024)
    swaps = []
    for p in range(patches - 1):
        left, right = p * GROUPS + GROUPS - 1, (p + 1) * GROUPS
        swaps += [(left, right), (right, left)]
    rim = lax.ppermute(positions, ("patch", "elem"), swaps)
    packed = pl.pallas_call(
        pack_kernel, out_shape=shape(GROUPS, PACKED, LANES),
        in_specs=vmem(5) + [pl.BlockSpec(memory_space=pltpu.SMEM)] + vmem(1), out_specs=vmem(1)[0],
        name="pack",
    )(positions, target, inertia, incidence, rest_inverse, counts, rim)
    whole = lax.all_to_all(packed, "elem", 0, 0, tiled=True).reshape(GROUPS * PACKED, LANES)
    wide = 3 * ROWS
    factors, first, image, diagonal, up, down = pl.pallas_call(
        setup_kernel,
        out_shape=[shape(81 * TRI_ROWS, LANES), shape(wide, LANES), shape(wide, LANES), shape(wide, LANES),
                   shape(16, LANES), shape(16, LANES)],
        in_specs=vmem(5), out_specs=vmem(6),
        scratch_shapes=[pltpu.VMEM((wide, LANES), F32), pltpu.VMEM((GROUPS * 16, LANES), F32),
                        pltpu.VMEM((LANES, 16), F32), pltpu.VMEM((96, LANES), F32),
                        pltpu.VMEM((96 * GROUPS, LANES), F32), pltpu.VMEM((14 * GROUPS, LANES), F32),
                        pltpu.VMEM((12 * ROWS, LANES), F32)],
        compiler_params=params, name="setup",
    )(whole, w_in, w_hid1, w_hid2, w_out)
    above = lax.ppermute(up, "patch", [(p, p + 1) for p in range(patches - 1)])
    below = lax.ppermute(down, "patch", [(p + 1, p) for p in range(patches - 1)])
    second, third, last_image, sums = pl.pallas_call(
        krylov_kernel,
        out_shape=[shape(wide, LANES), shape(wide, LANES), shape(wide, LANES), shape(patches, LANES)],
        in_specs=vmem(7), out_specs=vmem(4),
        scratch_shapes=[pltpu.VMEM((8 * GROUPS, LANES), F32), pltpu.VMEM((6 * ROWS, LANES), F32)],
        compiler_params=params, name="krylov",
    )(whole, factors, first, image, diagonal, above, below)
    sums = lax.all_to_all(sums, "patch", 0, 0, tiled=True)
    return pl.pallas_call(
        finish_kernel, out_shape=[shape(*positions.shape)] * 2,
        in_specs=vmem(6), out_specs=vmem(2), compiler_params=params, name="finish",
    )(sums, first, second, third, last_image, diagonal)


def solution(mesh):
    split = P(None, ("patch", "elem"))
    placed = (split,) * 5 + (P(("patch", "elem")),) + (P(),) * 4
    return jax.shard_map(per_device, mesh=mesh, in_specs=placed, out_specs=(split, split), check_vma=False)
```

```python
import functools

import jax
import jax.numpy as jnp
from jax import lax
from jax.experimental import pallas as pl
from jax.experimental.pallas import tpu as pltpu
from jax.sharding import PartitionSpec as P

STIFF = 1.0
REG = 0.1
GROUPS = 8
LANES = 128
TRI_CHUNKS = 6
VERT_CHUNKS = 2
ROWS = VERT_CHUNKS * GROUPS
TRI_ROWS = TRI_CHUNKS * GROUPS

POS, TGT, INERTIA, COUNT, INC, RINV, RIM, PACKED = 0, 6, 12, 14, 16, 34, 58, 64

HID1, HID2, LAST, WEIGHTS = 16, 144, 272, 368

F32 = jnp.float32
BF16 = jnp.bfloat16


def vmem(n):
    return [pl.BlockSpec(memory_space=pltpu.VMEM)] * n


def iota(shape, axis):
    return lax.broadcasted_iota(jnp.int32, shape, axis)


def pack_kernel(pos, tgt, inertia, inc, rinv, counts, w_in, w_hid1, w_hid2, w_out, rim, out, weights):
    first = lax.axis_index("elem") == 0
    weights[0:16] = jnp.concatenate([w_in[...].astype(F32), jnp.zeros((10, LANES), F32)], axis=0).astype(BF16)
    weights[HID1:HID2] = w_hid1[...]
    weights[HID2:LAST] = w_hid2[...]
    weights[LAST:WEIGHTS] = jnp.concatenate([w_out[...].astype(F32), jnp.zeros((6, LANES), F32)], axis=0).astype(BF16)
    out[0] = jnp.zeros((PACKED, LANES), F32)
    for k in range(VERT_CHUNKS):
        cut = slice(k * LANES, (k + 1) * LANES)
        out[0, POS + 3 * k : POS + 3 * k + 3] = pos[:, cut]
        out[0, TGT + 3 * k : TGT + 3 * k + 3] = tgt[:, cut]
        out[0, INERTIA + k : INERTIA + k + 1] = inertia[:, cut]
    out[0, COUNT : COUNT + 1] = jnp.full((1, LANES), counts[0], jnp.int32).astype(F32)
    for k in range(TRI_CHUNKS):
        cut = slice(k * LANES, (k + 1) * LANES)
        out[0, INC + 3 * k : INC + 3 * k + 3] = inc[:, cut].astype(F32)
        out[0, RINV + 4 * k : RINV + 4 * k + 4] = rinv[:, cut]
    out[0, RIM : RIM + 3] = jnp.where(first, rim[:, LANES:], rim[:, :LANES])
    block = out[0]
    for e in range(1, GROUPS):
        out[e] = block


def lane_rows(ref, row):
    return ref[pl.ds(row, GROUPS, stride=PACKED), :]


def corner_of(whole, k, q):
    index = lane_rows(whole, INC + 3 * k + q).astype(jnp.int32)
    row = ((index >> 7) & 1) * GROUPS + (index >> 8)
    return row, index & (LANES - 1)


def valid_of(whole, k):
    slot = iota((GROUPS, LANES), 1) + k * LANES
    return (slot.astype(F32) < lane_rows(whole, COUNT)).astype(F32)


def one_hot(row, lane, q, k, hot_lane, hot_row, stage):
    stage[0:8] = row.astype(F32)
    stage[8:16] = lane.astype(F32)
    places = iota((LANES, LANES), 0).astype(F32)
    for e in range(GROUPS):
        at = q * GROUPS * LANES + e * LANES
        for ref, first, count in ((hot_row, e, ROWS), (hot_lane, 8 + e, LANES)):
            line = jnp.broadcast_to(stage[first : first + 1, :], (count, LANES))
            ref[k, :, at : at + LANES] = jnp.where(line == places[:count], 1.0, 0.0).astype(BF16)


def gather(field, places):
    found = [[jnp.zeros((GROUPS, LANES), F32)] * 3 for _ in places]
    for h in range(ROWS):
        here = [row == h for row, _ in places]
        for c in range(3):
            line = jnp.broadcast_to(field[c * ROWS + h : c * ROWS + h + 1, :], (GROUPS, LANES))
            for q, (_, lane) in enumerate(places):
                value = jnp.take_along_axis(line, lane, axis=1, mode="promise_in_bounds")
                found[q][c] = jnp.where(here[q], value, found[q][c])
    return found


def spread_out(values, k, hot_row, stage, spread):
    comps = len(values[0])
    for q in range(3):
        for c, value in enumerate(values[q]):
            upper = value.astype(BF16).astype(F32)
            stage[q, 8 * c : 8 * c + 8] = upper
            stage[q, 8 * (comps + c) : 8 * (comps + c) + 8] = value - upper
        for e in range(GROUPS):
            at = q * GROUPS * LANES + e * LANES
            mask = hot_row[k, :, at : at + LANES]
            for c in range(2 * comps):
                line = jnp.broadcast_to(stage[q, 8 * c + e : 8 * c + e + 1, :], (ROWS, LANES)).astype(BF16)
                spread[ROWS * c : ROWS * (c + 1), at : at + LANES] = line * mask


def collect(spread, k, hot_lane):
    return lax.dot_general(spread[...], hot_lane[k], (((1,), (1,)), ((), ())), preferred_element_type=F32)


def sweep(build, hot_lane, spreads, total):
    total[...] = jnp.zeros_like(total)
    spreads[1][...] = jnp.zeros_like(spreads[1])

    @pl.loop(0, TRI_CHUNKS // 2)
    def _(i):
        for half in range(2):
            k = 2 * i + half
            part = collect(spreads[1 - half], jnp.maximum(k - 1, 0), hot_lane)
            build(k, spreads[half])
            total[...] += part

    half = total.shape[0] // 2
    whole = total[...] + collect(spreads[1], TRI_CHUNKS - 1, hot_lane)
    total[0:half] = whole[:half] + whole[half:]


def chain(here, before=None, after=None):
    lane = iota((GROUPS, LANES), 1)
    sub = iota((GROUPS, LANES), 0)
    low, high = here
    low_up, high_up = pltpu.roll(low, 1, 1), pltpu.roll(high, 1, 1)
    low_down, high_down = pltpu.roll(low, LANES - 1, 1), pltpu.roll(high, LANES - 1, 1)
    edge = 0.0 if before is None else pltpu.roll(jnp.broadcast_to(before, (GROUPS, LANES)), 1, 1)
    rim = jnp.where(sub == 0, edge, pltpu.roll(high_up, 1, 0))
    before_low = jnp.where(lane == 0, rim, low_up)
    before_high = jnp.where(lane == 0, low_up, high_up)
    edge = 0.0 if after is None else pltpu.roll(jnp.broadcast_to(after, (GROUPS, LANES)), LANES - 1, 1)
    rim = jnp.where(sub == GROUPS - 1, edge, pltpu.roll(low_down, GROUPS - 1, 0))
    after_low = jnp.where(lane == LANES - 1, high_down, low_down)
    after_high = jnp.where(lane == LANES - 1, rim, high_down)
    return (STIFF * (2.0 * low - before_low - after_low), STIFF * (2.0 * high - before_high - after_high))


def chunks(ref, c):
    at = c * ROWS
    return ref[at : at + GROUPS, :], ref[at + GROUPS : at + ROWS, :]


def put(ref, c, pair):
    at = c * ROWS
    ref[at : at + GROUPS, :] = pair[0]
    ref[at + GROUPS : at + ROWS, :] = pair[1]


def elements(whole, factors, hot_lane, hot_row, field, stage, spreads, total):
    def build(k, spread):
        found = gather(field, [corner_of(whole, k, q) for q in range(3)])
        u = found[0] + found[1] + found[2]

        def factor(j, m):
            return factors[pl.ds(pl.multiple_of((9 * j + m) * TRI_ROWS + k * GROUPS, GROUPS), GROUPS), :]

        inner = [sum(factor(j, m) * u[j] for j in range(9)) * (1.0 / 9.0) for m in range(9)]
        shift = REG * valid_of(whole, k)
        out = [sum(factor(j, m) * inner[m] for m in range(9)) + shift * u[j] for j in range(9)]
        spread_out([out[0:3], out[3:6], out[6:9]], k, hot_row, stage, spread)

    sweep(build, hot_lane, spreads, total)


def inertia_of(whole):
    return [lane_rows(whole, INERTIA + k) for k in range(VERT_CHUNKS)]


def apply_local(whole, factors, hots, field, stage, spreads, total, befores=None, afters=None):
    elements(whole, factors, *hots, field, stage, spreads, total)
    mass = inertia_of(whole)
    out = []
    for c in range(3):
        v = chunks(field, c)
        bent = chain(v, befores and befores[c], afters and afters[c])
        felt = chunks(total, c)
        out.append([mass[k] * v[k] + bent[k] + felt[k] for k in range(VERT_CHUNKS)])
    return out


def setup_kernel(whole, weights, factors, hot_lane, hot_row, first, image, diagonal, up, down,
                 pos, feats, inputs, outputs, raw, stage6, spread6a, spread6b, total6,
                 stage, spread_a, spread_b, total):
    for c in range(3):
        put(pos, c, [lane_rows(whole, POS + 3 * k + c) for k in range(VERT_CHUNKS)])
    feats[...] = jnp.zeros_like(feats)

    @pl.loop(0, TRI_CHUNKS)
    def _(k):
        places = [corner_of(whole, k, q) for q in range(3)]
        for q, (row, lane) in enumerate(places):
            one_hot(row, lane, q, k, hot_lane, hot_row, stage.at[q])
        x0, x1, x2 = gather(pos, places)
        a, b, c_, d = [lane_rows(whole, RINV + 4 * k + i) for i in range(4)]
        for c in range(3):
            one, two = x1[c] - x0[c], x2[c] - x0[c]
            feats[pl.ds(c, GROUPS, stride=16), :] = one * a + two * c_
            feats[pl.ds(3 + c, GROUPS, stride=16), :] = one * b + two * d
        inputs[k] = jnp.concatenate([feats[16 * e : 16 * e + 16, :] for e in range(GROUPS)], axis=1).astype(BF16)

    x = jnp.concatenate([inputs[k] for k in range(TRI_CHUNKS)], axis=1)
    h = lax.dot_general(weights[0:HID1], x, (((0,), (0,)), ((), ())), preferred_element_type=F32)
    h = jnp.tanh(h).astype(BF16)
    for weight in (weights[HID1:HID2], weights[HID2:LAST]):
        h = jnp.tanh(jnp.dot(weight, h, preferred_element_type=F32)).astype(BF16)
    o = jnp.dot(weights[LAST:WEIGHTS], h, preferred_element_type=F32)
    for k in range(TRI_CHUNKS):
        outputs[k] = o[:, k * GROUPS * LANES : (k + 1) * GROUPS * LANES]

    def build(k, spread):
        for e in range(GROUPS):
            for g in range(12):
                raw[pl.ds(g * 64 + e, 8, stride=8), :] = outputs[k, 8 * g : 8 * g + 8, e * LANES : (e + 1) * LANES]
        valid = valid_of(whole, k)
        forces, curves = [], []
        for j in range(9):
            forces.append(raw[8 * j : 8 * j + 8, :] * valid)
            curve = 0.0
            for m in range(9):
                at = 9 * j + m
                g = (raw[8 * (9 + at) : 8 * (9 + at) + 8, :] * valid).astype(BF16).astype(F32)
                factors[pl.ds(pl.multiple_of(at * TRI_ROWS + k * GROUPS, GROUPS), GROUPS), :] = g
                curve += g * g
            curves.append(curve * (1.0 / 9.0) + REG * valid)
        values = [forces[3 * q : 3 * q + 3] + curves[3 * q : 3 * q + 3] for q in range(3)]
        spread_out(values, k, hot_row, stage6, spread)

    sweep(build, hot_lane, (spread6a, spread6b), total6)
    mass = inertia_of(whole)
    inverse = []
    for c in range(3):
        x = chunks(pos, c)
        bent = chain(x, whole[RIM + c : RIM + c + 1, :],
                     whole[(GROUPS - 1) * PACKED + RIM + c : (GROUPS - 1) * PACKED + RIM + c + 1, :])
        felt, curve = chunks(total6, c), chunks(total6, 3 + c)
        diag = [mass[k] + curve[k] + 2.0 * STIFF for k in range(VERT_CHUNKS)]
        inv = [1.0 / diag[k] for k in range(VERT_CHUNKS)]
        grad = [mass[k] * (x[k] - lane_rows(whole, TGT + 3 * k + c)) + bent[k] + felt[k]
                for k in range(VERT_CHUNKS)]
        put(diagonal, c, diag)
        put(first, c, [-grad[k] * inv[k] for k in range(VERT_CHUNKS)])
        inverse.append(inv)
    w = apply_local(whole, factors, (hot_lane, hot_row), first, stage, (spread_a, spread_b), total)
    up[...] = jnp.zeros_like(up)
    down[...] = jnp.zeros_like(down)
    for c in range(3):
        v = chunks(first, c)
        put(image, c, w[c])
        nxt = [w[c][k] * inverse[c][k] - v[k] for k in range(VERT_CHUNKS)]
        for i, what in enumerate((v, nxt, inverse[c])):
            up[3 * i + c : 3 * i + c + 1, :] = what[1][GROUPS - 1 : GROUPS, :]
            down[3 * i + c : 3 * i + c + 1, :] = what[0][0:1, :]


def krylov_kernel(whole, factors, hot_lane, hot_row, first, image, diagonal, above, below,
                  second, third, last_image, sums, stage, spread_a, spread_b, total):
    hots, spreads = (hot_lane, hot_row), (spread_a, spread_b)
    lane = iota((GROUPS, LANES), 1)
    sub = iota((GROUPS, LANES), 0)
    head = (lane == 0) & (sub == 0)
    tail = (lane == LANES - 1) & (sub == GROUPS - 1)

    def spread(row):
        return jnp.broadcast_to(row, (GROUPS, LANES))

    befores, afters = [], []
    for c in range(3):
        v0, w0 = chunks(first, c), chunks(image, c)
        diag = chunks(diagonal, c)
        inv = [1.0 / diag[k] for k in range(VERT_CHUNKS)]
        old_up, old_down = above[c : c + 1, :], below[c : c + 1, :]
        w_low = w0[0] - STIFF * jnp.where(head, pltpu.roll(spread(old_up), 1, 1), 0.0)
        w_high = w0[1] - STIFF * jnp.where(tail, pltpu.roll(spread(old_down), LANES - 1, 1), 0.0)
        put(second, c, [w_low * inv[0] - v0[0], w_high * inv[1] - v0[1]])
        mine_low = pltpu.roll(spread(v0[0][0:1, :]), LANES - 1, 1)[0:1, :]
        mine_high = pltpu.roll(spread(v0[1][GROUPS - 1 : GROUPS, :]), 1, 1)[0:1, :]
        befores.append(above[3 + c : 4 + c, :] - STIFF * mine_low * above[6 + c : 7 + c, :])
        afters.append(below[3 + c : 4 + c, :] - STIFF * mine_high * below[6 + c : 7 + c, :])
    w = apply_local(whole, factors, hots, second, stage, spreads, total, befores, afters)
    for c in range(3):
        diag, v1 = chunks(diagonal, c), chunks(second, c)
        put(third, c, [w[c][k] / diag[k] - v1[k] for k in range(VERT_CHUNKS)])
    w = apply_local(whole, factors, hots, third, stage, spreads, total)
    moment = [0.0] * 6
    ends = []
    for c in range(3):
        put(last_image, c, w[c])
        diag = chunks(diagonal, c)
        v0, v1, v2 = chunks(first, c), chunks(second, c), chunks(third, c)
        for k in range(VERT_CHUNKS):
            m0, m1, m2 = diag[k] * v0[k], diag[k] * v1[k], diag[k] * v2[k]
            for i, term in enumerate((m0 * v0[k], m0 * v1[k], m1 * v1[k], m1 * v2[k], m2 * v2[k],
                                      v2[k] * w[c][k] - m2 * v2[k])):
                moment[i] += term
        ends.append((jnp.where(head, v2[0], 0.0), jnp.where(tail, v2[1], 0.0)))
    line = jnp.zeros((1, LANES), F32)
    for i, part in enumerate(moment + [x[0] for x in ends] + [x[1] for x in ends]):
        value = jnp.sum(jnp.sum(part, axis=0, keepdims=True), axis=1, keepdims=True)
        line = jnp.where(iota((1, LANES), 1) == i, value, line)
    sums[...] = jnp.broadcast_to(line, sums.shape)


def finish_kernel(sums, first, second, third, last_image, diagonal, field, residual):
    patch, elem = lax.axis_index("patch"), lax.axis_index("elem")
    patches = sums.shape[0]
    every = sums[...]
    lane = iota(every.shape, 1)
    sub = iota(every.shape, 0)
    totals = jnp.sum(every, axis=0, keepdims=True)

    def pick(row, i):
        return jnp.sum(jnp.where(iota((1, LANES), 1) == i, row, 0.0), axis=1, keepdims=True)

    after = pltpu.roll(pltpu.roll(every, patches - 1, 0), 3, 1)
    coupled = jnp.where((lane >= 9) & (lane < 12) & (sub < patches - 1), every * after, 0.0)
    coupling = jnp.sum(jnp.sum(coupled, axis=0, keepdims=True), axis=1, keepdims=True)
    mu = [pick(totals, i) for i in range(6)]
    mu[5] = mu[5] - 2.0 * STIFF * coupling

    def inner(p, q):
        return sum(a * b * mu[i + j] for i, a in enumerate(p) for j, b in enumerate(q))

    def applied(p):
        padded = list(p) + [0.0 * mu[0]]
        return [padded[0]] + [padded[j] + padded[j - 1] for j in range(1, len(padded))]

    one = jnp.ones((1, 1), F32)
    z, direction, x = [one], [one], []
    rz = inner(z, z)
    for step in range(3):
        ahead = applied(direction)
        alpha = rz / inner(direction, ahead)
        x = [(x[j] if j < len(x) else 0.0) + alpha * direction[j] for j in range(len(direction))]
        z = [(z[j] if j < len(z) else 0.0) - alpha * ahead[j] for j in range(len(ahead))]
        if step < 2:
            new = inner(z, z)
            ratio = new / rz
            direction = [z[j] + (ratio * direction[j] if j < len(direction) else 0.0) for j in range(len(z))]
            rz = new
    place = iota((1, LANES), 1)
    prev = sums[pl.ds(jnp.maximum(patch - 1, 0), 1), :]
    nxt = sums[pl.ds(jnp.minimum(patch + 1, patches - 1), 1), :]
    at_head = (place == 0) & (elem == 0) & (patch > 0)
    at_tail = (place == LANES - 1) & (elem == GROUPS - 1) & (patch < patches - 1)
    for c in range(3):
        for k in range(VERT_CHUNKS):
            at = pl.ds(c * ROWS + k * GROUPS + elem, 1)
            v0, v1, v2, w2, diag = first[at, :], second[at, :], third[at, :], last_image[at, :], diagonal[at, :]
            if k == 0:
                w2 = w2 - STIFF * jnp.where(at_head, pick(prev, 9 + c), 0.0)
            else:
                w2 = w2 - STIFF * jnp.where(at_tail, pick(nxt, 6 + c), 0.0)
            v3 = w2 / diag - v2
            cut = slice(k * LANES, (k + 1) * LANES)
            field[c : c + 1, cut] = x[0] * v0 + x[1] * v1 + x[2] * v2
            residual[c : c + 1, cut] = diag * (z[0] * v0 + z[1] * v1 + z[2] * v2 + z[3] * v3)


def shape(*dims):
    return jax.ShapeDtypeStruct(dims, F32)


def per_device(positions, target, inertia, incidence, rest_inverse, counts, w_in, w_hid1, w_hid2, w_out):
    patches = lax.axis_size("patch")
    params = pltpu.CompilerParams(vmem_limit_bytes=16 * 1024 * 1024)
    swaps = []
    for p in range(patches - 1):
        left, right = p * GROUPS + GROUPS - 1, (p + 1) * GROUPS
        swaps += [(left, right), (right, left)]
    rim = lax.ppermute(positions, ("patch", "elem"), swaps)
    packed, weights = pl.pallas_call(
        pack_kernel, out_shape=[shape(GROUPS, PACKED, LANES), jax.ShapeDtypeStruct((WEIGHTS, LANES), BF16)],
        in_specs=vmem(5) + [pl.BlockSpec(memory_space=pltpu.SMEM)] + vmem(5), out_specs=vmem(2),
        name="pack",
    )(positions, target, inertia, incidence, rest_inverse, counts, w_in.T, w_hid1, w_hid2, w_out, rim)
    whole = lax.all_to_all(packed, "elem", 0, 0, tiled=True).reshape(GROUPS * PACKED, LANES)
    wide = 3 * ROWS
    width = GROUPS * LANES

    def scatter_scratch(comps):
        spread = pltpu.VMEM((2 * comps * ROWS, 3 * width), BF16)
        return [pltpu.VMEM((3, 2 * comps * GROUPS, LANES), F32), spread, spread,
                pltpu.VMEM((2 * comps * ROWS, LANES), F32)]

    factors, hot_lane, hot_row, first, image, diagonal, up, down = pl.pallas_call(
        setup_kernel,
        out_shape=[shape(81 * TRI_ROWS, LANES), jax.ShapeDtypeStruct((TRI_CHUNKS, LANES, 3 * width), BF16),
                   jax.ShapeDtypeStruct((TRI_CHUNKS, ROWS, 3 * width), BF16),
                   shape(wide, LANES), shape(wide, LANES), shape(wide, LANES), shape(16, LANES), shape(16, LANES)],
        in_specs=vmem(2), out_specs=vmem(8),
        scratch_shapes=[pltpu.VMEM((wide, LANES), F32), pltpu.VMEM((GROUPS * 16, LANES), F32),
                        pltpu.VMEM((TRI_CHUNKS, 16, width), BF16), pltpu.VMEM((TRI_CHUNKS, 96, width), F32),
                        pltpu.VMEM((96 * GROUPS, LANES), F32)] + scatter_scratch(6) + scatter_scratch(3),
        compiler_params=params, name="setup",
    )(whole, weights)
    above = lax.ppermute(up, "patch", [(p, p + 1) for p in range(patches - 1)])
    below = lax.ppermute(down, "patch", [(p + 1, p) for p in range(patches - 1)])
    second, third, last_image, sums = pl.pallas_call(
        krylov_kernel,
        out_shape=[shape(wide, LANES), shape(wide, LANES), shape(wide, LANES), shape(patches, LANES)],
        in_specs=vmem(9), out_specs=vmem(4), scratch_shapes=scatter_scratch(3),
        compiler_params=params, name="krylov",
    )(whole, factors, hot_lane, hot_row, first, image, diagonal, above, below)
    sums = lax.all_to_all(sums, "patch", 0, 0, tiled=True)
    return pl.pallas_call(
        finish_kernel, out_shape=[shape(*positions.shape)] * 2,
        in_specs=vmem(6), out_specs=vmem(2), compiler_params=params, name="finish",
    )(sums, first, second, third, last_image, diagonal)


def solution(mesh):
    split = P(None, ("patch", "elem"))
    placed = (split,) * 5 + (P(("patch", "elem")),) + (P(),) * 4
    return jax.shard_map(per_device, mesh=mesh, in_specs=placed, out_specs=(split, split), check_vma=False)
```

```python
import functools

import jax
import jax.numpy as jnp
from jax import lax
from jax.experimental import pallas as pl
from jax.experimental.pallas import tpu as pltpu
from jax.sharding import PartitionSpec as P

STIFF = 1.0
REG = 0.1
GROUPS = 8
LANES = 128
TRI_CHUNKS = 6
VERT_CHUNKS = 2
ROWS = VERT_CHUNKS * GROUPS
TRI_ROWS = TRI_CHUNKS * GROUPS

POS, TGT, INERTIA, COUNT, INC, RINV, RIM, PACKED = 0, 6, 12, 14, 16, 34, 58, 64

HID1, HID2, LAST, WEIGHTS = 16, 144, 272, 368

SHARED = 16

F32 = jnp.float32
BF16 = jnp.bfloat16


def vmem(n):
    return [pl.BlockSpec(memory_space=pltpu.VMEM)] * n


def iota(shape, axis):
    return lax.broadcasted_iota(jnp.int32, shape, axis)


def pack_kernel(pos, tgt, inertia, inc, rinv, counts, w_in, w_hid1, w_hid2, w_out, rim, out, weights):
    first = lax.axis_index("elem") == 0
    weights[0:16] = jnp.concatenate([w_in[...].astype(F32), jnp.zeros((10, LANES), F32)], axis=0).astype(BF16)
    weights[HID1:HID2] = w_hid1[...]
    weights[HID2:LAST] = w_hid2[...]
    weights[LAST:WEIGHTS] = jnp.concatenate([w_out[...].astype(F32), jnp.zeros((6, LANES), F32)], axis=0).astype(BF16)
    out[0] = jnp.zeros((PACKED, LANES), F32)
    for k in range(VERT_CHUNKS):
        cut = slice(k * LANES, (k + 1) * LANES)
        out[0, POS + 3 * k : POS + 3 * k + 3] = pos[:, cut]
        out[0, TGT + 3 * k : TGT + 3 * k + 3] = tgt[:, cut]
        out[0, INERTIA + k : INERTIA + k + 1] = inertia[:, cut]
    out[0, COUNT : COUNT + 1] = jnp.full((1, LANES), counts[0], jnp.int32).astype(F32)
    for k in range(TRI_CHUNKS):
        cut = slice(k * LANES, (k + 1) * LANES)
        out[0, INC + 3 * k : INC + 3 * k + 3] = inc[:, cut].astype(F32)
        out[0, RINV + 4 * k : RINV + 4 * k + 4] = rinv[:, cut]
    out[0, RIM : RIM + 3] = jnp.where(first, rim[:, LANES:], rim[:, :LANES])
    block = out[0]
    for e in range(1, GROUPS):
        out[e] = block


def lane_rows(ref, row):
    return ref[pl.ds(row, GROUPS, stride=PACKED), :]


def corner_of(whole, k, q):
    index = lane_rows(whole, INC + 3 * k + q).astype(jnp.int32)
    row = ((index >> 7) & 1) * GROUPS + (index >> 8)
    return row, index & (LANES - 1)


def valid_of(whole, k):
    slot = iota((GROUPS, LANES), 1) + k * LANES
    return (slot.astype(F32) < lane_rows(whole, COUNT)).astype(F32)


def one_hot(row, lane, q, k, hot_lane, hot_row, stage):
    stage[0:8] = row.astype(F32)
    stage[8:16] = lane.astype(F32)
    places = iota((LANES, LANES), 0).astype(F32)
    for e in range(GROUPS):
        at = q * GROUPS * LANES + e * LANES
        for ref, first, count in ((hot_row, e, ROWS), (hot_lane, 8 + e, LANES)):
            line = jnp.broadcast_to(stage[first : first + 1, :], (count, LANES))
            ref[k, :, at : at + LANES] = jnp.where(line == places[:count], 1.0, 0.0).astype(BF16)


def gather(field, places):
    found = [[jnp.zeros((GROUPS, LANES), F32)] * 3 for _ in places]
    for h in range(ROWS):
        here = [row == h for row, _ in places]
        for c in range(3):
            line = jnp.broadcast_to(field[c * ROWS + h : c * ROWS + h + 1, :], (GROUPS, LANES))
            for q, (_, lane) in enumerate(places):
                value = jnp.take_along_axis(line, lane, axis=1, mode="promise_in_bounds")
                found[q][c] = jnp.where(here[q], value, found[q][c])
    return found


def spread_out(values, k, hot_row, stage, spread):
    comps = len(values[0])
    for q in range(3):
        for c, value in enumerate(values[q]):
            upper = value.astype(BF16).astype(F32)
            stage[q, 8 * c : 8 * c + 8] = upper
            stage[q, 8 * (comps + c) : 8 * (comps + c) + 8] = value - upper
        for e in range(GROUPS):
            at = q * GROUPS * LANES + e * LANES
            mask = hot_row[k, :, at : at + LANES]
            for c in range(2 * comps):
                line = jnp.broadcast_to(stage[q, 8 * c + e : 8 * c + e + 1, :], (ROWS, LANES)).astype(BF16)
                spread[ROWS * c : ROWS * (c + 1), at : at + LANES] = line * mask


def collect(spread, k, hot_lane):
    return lax.dot_general(spread[...], hot_lane[k], (((1,), (1,)), ((), ())), preferred_element_type=F32)


def sweep(build, hot_lane, spreads, total):
    total[...] = jnp.zeros_like(total)
    for k in range(TRI_CHUNKS):
        if k > 0:
            total[...] += collect(spreads[(k - 1) % 2], k - 1, hot_lane)
        build(k, spreads[k % 2], k % 2)
    half = total.shape[0] // 2
    whole = total[...] + collect(spreads[(TRI_CHUNKS - 1) % 2], TRI_CHUNKS - 1, hot_lane)
    total[0:half] = whole[:half] + whole[half:]


def chain(here, before=None, after=None):
    lane = iota((GROUPS, LANES), 1)
    sub = iota((GROUPS, LANES), 0)
    low, high = here
    low_up, high_up = pltpu.roll(low, 1, 1), pltpu.roll(high, 1, 1)
    low_down, high_down = pltpu.roll(low, LANES - 1, 1), pltpu.roll(high, LANES - 1, 1)
    edge = 0.0 if before is None else pltpu.roll(jnp.broadcast_to(before, (GROUPS, LANES)), 1, 1)
    rim = jnp.where(sub == 0, edge, pltpu.roll(high_up, 1, 0))
    before_low = jnp.where(lane == 0, rim, low_up)
    before_high = jnp.where(lane == 0, low_up, high_up)
    edge = 0.0 if after is None else pltpu.roll(jnp.broadcast_to(after, (GROUPS, LANES)), LANES - 1, 1)
    rim = jnp.where(sub == GROUPS - 1, edge, pltpu.roll(low_down, GROUPS - 1, 0))
    after_low = jnp.where(lane == LANES - 1, high_down, low_down)
    after_high = jnp.where(lane == LANES - 1, rim, high_down)
    return (STIFF * (2.0 * low - before_low - after_low), STIFF * (2.0 * high - before_high - after_high))


def chunks(ref, c):
    at = c * ROWS
    return ref[at : at + GROUPS, :], ref[at + GROUPS : at + ROWS, :]


def put(ref, c, pair):
    at = c * ROWS
    ref[at : at + GROUPS, :] = pair[0]
    ref[at + GROUPS : at + ROWS, :] = pair[1]


def elements(whole, factors, hot_lane, hot_row, field, stage, spreads, total):
    def find(k):
        return gather(field, [corner_of(whole, k, q) for q in range(3)])

    ahead = [find(0)]

    def build(k, spread, turn):
        found = ahead.pop()
        u = found[0] + found[1] + found[2]
        if k + 1 < TRI_CHUNKS:
            ahead.append(find(k + 1))

        def factor(j, m):
            return factors[pl.ds(pl.multiple_of((9 * j + m) * TRI_ROWS + k * GROUPS, GROUPS), GROUPS), :]

        inner = [sum(factor(j, m) * u[j] for j in range(9)) * (1.0 / 9.0) for m in range(9)]
        shift = REG * valid_of(whole, k)
        out = [sum(factor(j, m) * inner[m] for m in range(9)) + shift * u[j] for j in range(9)]
        spread_out([out[0:3], out[3:6], out[6:9]], k, hot_row, stage.at[turn], spread)

    sweep(build, hot_lane, spreads, total)


def inertia_of(whole):
    return [lane_rows(whole, INERTIA + k) for k in range(VERT_CHUNKS)]


def apply_local(whole, factors, hots, field, stage, spreads, total, befores=None, afters=None):
    elements(whole, factors, *hots, field, stage, spreads, total)
    mass = inertia_of(whole)
    out = []
    for c in range(3):
        v = chunks(field, c)
        bent = chain(v, befores and befores[c], afters and afters[c])
        felt = chunks(total, c)
        out.append([mass[k] * v[k] + bent[k] + felt[k] for k in range(VERT_CHUNKS)])
    return out


def setup_kernel(whole, weights, factors, hot_lane, hot_row, first, image, diagonal, up, down,
                 pos, feats, inputs, outputs, raw, stage6, spread6a, spread6b, total6,
                 stage, spread_a, spread_b, total):
    for c in range(3):
        put(pos, c, [lane_rows(whole, POS + 3 * k + c) for k in range(VERT_CHUNKS)])
    feats[...] = jnp.zeros_like(feats)

    @pl.loop(0, TRI_CHUNKS)
    def _(k):
        places = [corner_of(whole, k, q) for q in range(3)]
        for q, (row, lane) in enumerate(places):
            one_hot(row, lane, q, k, hot_lane, hot_row, stage.at[0, q])
        x0, x1, x2 = gather(pos, places)
        a, b, c_, d = [lane_rows(whole, RINV + 4 * k + i) for i in range(4)]
        for c in range(3):
            one, two = x1[c] - x0[c], x2[c] - x0[c]
            feats[pl.ds(c, GROUPS, stride=16), :] = one * a + two * c_
            feats[pl.ds(3 + c, GROUPS, stride=16), :] = one * b + two * d
        inputs[k] = jnp.concatenate([feats[16 * e : 16 * e + 16, :] for e in range(GROUPS)], axis=1).astype(BF16)

    x = jnp.concatenate([inputs[k] for k in range(TRI_CHUNKS)], axis=1)
    h = lax.dot_general(weights[0:HID1], x, (((0,), (0,)), ((), ())), preferred_element_type=F32)
    h = jnp.tanh(h).astype(BF16)
    for weight in (weights[HID1:HID2], weights[HID2:LAST]):
        h = jnp.tanh(jnp.dot(weight, h, preferred_element_type=F32)).astype(BF16)
    o = jnp.dot(weights[LAST:WEIGHTS], h, preferred_element_type=F32)
    for k in range(TRI_CHUNKS):
        outputs[k] = o[:, k * GROUPS * LANES : (k + 1) * GROUPS * LANES]

    def build(k, spread, turn):
        for e in range(GROUPS):
            for g in range(12):
                raw[pl.ds(g * 64 + e, 8, stride=8), :] = outputs[k, 8 * g : 8 * g + 8, e * LANES : (e + 1) * LANES]
        valid = valid_of(whole, k)
        forces, curves = [], []
        for j in range(9):
            forces.append(raw[8 * j : 8 * j + 8, :] * valid)
            curve = 0.0
            for m in range(9):
                at = 9 * j + m
                g = (raw[8 * (9 + at) : 8 * (9 + at) + 8, :] * valid).astype(BF16).astype(F32)
                factors[pl.ds(pl.multiple_of(at * TRI_ROWS + k * GROUPS, GROUPS), GROUPS), :] = g
                curve += g * g
            curves.append(curve * (1.0 / 9.0) + REG * valid)
        values = [forces[3 * q : 3 * q + 3] + curves[3 * q : 3 * q + 3] for q in range(3)]
        spread_out(values, k, hot_row, stage6.at[turn], spread)

    sweep(build, hot_lane, (spread6a, spread6b), total6)
    mass = inertia_of(whole)
    inverse = []
    for c in range(3):
        x = chunks(pos, c)
        bent = chain(x, whole[RIM + c : RIM + c + 1, :],
                     whole[(GROUPS - 1) * PACKED + RIM + c : (GROUPS - 1) * PACKED + RIM + c + 1, :])
        felt, curve = chunks(total6, c), chunks(total6, 3 + c)
        diag = [mass[k] + curve[k] + 2.0 * STIFF for k in range(VERT_CHUNKS)]
        inv = [1.0 / diag[k] for k in range(VERT_CHUNKS)]
        grad = [mass[k] * (x[k] - lane_rows(whole, TGT + 3 * k + c)) + bent[k] + felt[k]
                for k in range(VERT_CHUNKS)]
        put(diagonal, c, diag)
        put(first, c, [-grad[k] * inv[k] for k in range(VERT_CHUNKS)])
        inverse.append(inv)
    w = apply_local(whole, factors, (hot_lane, hot_row), first, stage, (spread_a, spread_b), total)
    up[...] = jnp.zeros_like(up)
    down[...] = jnp.zeros_like(down)
    for c in range(3):
        v = chunks(first, c)
        put(image, c, w[c])
        nxt = [w[c][k] * inverse[c][k] - v[k] for k in range(VERT_CHUNKS)]
        for i, what in enumerate((v, nxt, inverse[c])):
            up[3 * i + c : 3 * i + c + 1, :] = what[1][GROUPS - 1 : GROUPS, :]
            down[3 * i + c : 3 * i + c + 1, :] = what[0][0:1, :]


def krylov_kernel(whole, factors, hot_lane, hot_row, first, image, diagonal, above, below,
                  second, third, last_image, sums, stage, spread_a, spread_b, total):
    hots, spreads = (hot_lane, hot_row), (spread_a, spread_b)
    lane = iota((GROUPS, LANES), 1)
    sub = iota((GROUPS, LANES), 0)
    head = (lane == 0) & (sub == 0)
    tail = (lane == LANES - 1) & (sub == GROUPS - 1)

    def spread(row):
        return jnp.broadcast_to(row, (GROUPS, LANES))

    befores, afters = [], []
    for c in range(3):
        v0, w0 = chunks(first, c), chunks(image, c)
        diag = chunks(diagonal, c)
        inv = [1.0 / diag[k] for k in range(VERT_CHUNKS)]
        old_up, old_down = above[c : c + 1, :], below[c : c + 1, :]
        w_low = w0[0] - STIFF * jnp.where(head, pltpu.roll(spread(old_up), 1, 1), 0.0)
        w_high = w0[1] - STIFF * jnp.where(tail, pltpu.roll(spread(old_down), LANES - 1, 1), 0.0)
        put(second, c, [w_low * inv[0] - v0[0], w_high * inv[1] - v0[1]])
        mine_low = pltpu.roll(spread(v0[0][0:1, :]), LANES - 1, 1)[0:1, :]
        mine_high = pltpu.roll(spread(v0[1][GROUPS - 1 : GROUPS, :]), 1, 1)[0:1, :]
        befores.append(above[3 + c : 4 + c, :] - STIFF * mine_low * above[6 + c : 7 + c, :])
        afters.append(below[3 + c : 4 + c, :] - STIFF * mine_high * below[6 + c : 7 + c, :])
    w = apply_local(whole, factors, hots, second, stage, spreads, total, befores, afters)
    for c in range(3):
        diag, v1 = chunks(diagonal, c), chunks(second, c)
        put(third, c, [w[c][k] / diag[k] - v1[k] for k in range(VERT_CHUNKS)])
    w = apply_local(whole, factors, hots, third, stage, spreads, total)
    moment = [0.0] * 6
    ends = []
    for c in range(3):
        put(last_image, c, w[c])
        diag = chunks(diagonal, c)
        v0, v1, v2 = chunks(first, c), chunks(second, c), chunks(third, c)
        for k in range(VERT_CHUNKS):
            m0, m1, m2 = diag[k] * v0[k], diag[k] * v1[k], diag[k] * v2[k]
            for i, term in enumerate((m0 * v0[k], m0 * v1[k], m1 * v1[k], m1 * v2[k], m2 * v2[k],
                                      v2[k] * w[c][k] - m2 * v2[k])):
                moment[i] += term
        ends.append((jnp.where(head, v2[0], 0.0), jnp.where(tail, v2[1], 0.0)))
    line = jnp.zeros((1, LANES), F32)
    for i, part in enumerate(moment + [x[0] for x in ends] + [x[1] for x in ends]):
        value = jnp.sum(jnp.sum(part, axis=0, keepdims=True), axis=1, keepdims=True)
        line = jnp.where(iota((1, LANES), 1) == i, value, line)
    sums[...] = jnp.broadcast_to(line[:, 0:SHARED], sums.shape)


def finish_kernel(sums, first, second, third, last_image, diagonal, field, residual):
    patch, elem = lax.axis_index("patch"), lax.axis_index("elem")
    patches = sums.shape[0]
    every = sums[...]
    lane = iota(every.shape, 1)
    sub = iota(every.shape, 0)
    totals = jnp.sum(every, axis=0, keepdims=True)

    def pick(row, i):
        return row[:, i : i + 1]

    after = pltpu.roll(pltpu.roll(every, patches - 1, 0), 3, 1)
    coupled = jnp.where((lane >= 9) & (lane < 12) & (sub < patches - 1), every * after, 0.0)
    coupling = jnp.sum(jnp.sum(coupled, axis=0, keepdims=True), axis=1, keepdims=True)
    mu = [pick(totals, i) for i in range(6)]
    mu[5] = mu[5] - 2.0 * STIFF * coupling

    def inner(p, q):
        return sum(a * b * mu[i + j] for i, a in enumerate(p) for j, b in enumerate(q))

    def applied(p):
        padded = list(p) + [0.0 * mu[0]]
        return [padded[0]] + [padded[j] + padded[j - 1] for j in range(1, len(padded))]

    one = jnp.ones((1, 1), F32)
    z, direction, x = [one], [one], []
    rz = inner(z, z)
    for step in range(3):
        ahead = applied(direction)
        alpha = rz / inner(direction, ahead)
        x = [(x[j] if j < len(x) else 0.0) + alpha * direction[j] for j in range(len(direction))]
        z = [(z[j] if j < len(z) else 0.0) - alpha * ahead[j] for j in range(len(ahead))]
        if step < 2:
            new = inner(z, z)
            ratio = new / rz
            direction = [z[j] + (ratio * direction[j] if j < len(direction) else 0.0) for j in range(len(z))]
            rz = new
    place = iota((1, LANES), 1)
    prev = sums[pl.ds(jnp.maximum(patch - 1, 0), 1), :]
    nxt = sums[pl.ds(jnp.minimum(patch + 1, patches - 1), 1), :]
    at_head = (place == 0) & (elem == 0) & (patch > 0)
    at_tail = (place == LANES - 1) & (elem == GROUPS - 1) & (patch < patches - 1)
    for c in range(3):
        for k in range(VERT_CHUNKS):
            at = pl.ds(c * ROWS + k * GROUPS + elem, 1)
            v0, v1, v2, w2, diag = first[at, :], second[at, :], third[at, :], last_image[at, :], diagonal[at, :]
            if k == 0:
                w2 = w2 - STIFF * jnp.where(at_head, pick(prev, 9 + c), 0.0)
            else:
                w2 = w2 - STIFF * jnp.where(at_tail, pick(nxt, 6 + c), 0.0)
            v3 = w2 / diag - v2
            cut = slice(k * LANES, (k + 1) * LANES)
            field[c : c + 1, cut] = x[0] * v0 + x[1] * v1 + x[2] * v2
            residual[c : c + 1, cut] = diag * (z[0] * v0 + z[1] * v1 + z[2] * v2 + z[3] * v3)


def shape(*dims):
    return jax.ShapeDtypeStruct(dims, F32)


def per_device(positions, target, inertia, incidence, rest_inverse, counts, w_in, w_hid1, w_hid2, w_out):
    patches = lax.axis_size("patch")
    params = pltpu.CompilerParams(vmem_limit_bytes=16 * 1024 * 1024)
    swaps = []
    for p in range(patches - 1):
        left, right = p * GROUPS + GROUPS - 1, (p + 1) * GROUPS
        swaps += [(left, right), (right, left)]
    rim = lax.ppermute(positions, ("patch", "elem"), swaps)
    packed, weights = pl.pallas_call(
        pack_kernel, out_shape=[shape(GROUPS, PACKED, LANES), jax.ShapeDtypeStruct((WEIGHTS, LANES), BF16)],
        in_specs=vmem(5) + [pl.BlockSpec(memory_space=pltpu.SMEM)] + vmem(5), out_specs=vmem(2),
        name="pack",
    )(positions, target, inertia, incidence, rest_inverse, counts, w_in.T, w_hid1, w_hid2, w_out, rim)
    whole = lax.all_to_all(packed, "elem", 0, 0, tiled=True).reshape(GROUPS * PACKED, LANES)
    wide = 3 * ROWS
    width = GROUPS * LANES

    def scatter_scratch(comps):
        spread = pltpu.VMEM((2 * comps * ROWS, 3 * width), BF16)
        return [pltpu.VMEM((2, 3, 2 * comps * GROUPS, LANES), F32), spread, spread,
                pltpu.VMEM((2 * comps * ROWS, LANES), F32)]

    factors, hot_lane, hot_row, first, image, diagonal, up, down = pl.pallas_call(
        setup_kernel,
        out_shape=[shape(81 * TRI_ROWS, LANES), jax.ShapeDtypeStruct((TRI_CHUNKS, LANES, 3 * width), BF16),
                   jax.ShapeDtypeStruct((TRI_CHUNKS, ROWS, 3 * width), BF16),
                   shape(wide, LANES), shape(wide, LANES), shape(wide, LANES), shape(16, LANES), shape(16, LANES)],
        in_specs=vmem(2), out_specs=vmem(8),
        scratch_shapes=[pltpu.VMEM((wide, LANES), F32), pltpu.VMEM((GROUPS * 16, LANES), F32),
                        pltpu.VMEM((TRI_CHUNKS, 16, width), BF16), pltpu.VMEM((TRI_CHUNKS, 96, width), F32),
                        pltpu.VMEM((96 * GROUPS, LANES), F32)] + scatter_scratch(6) + scatter_scratch(3),
        compiler_params=params, name="setup",
    )(whole, weights)
    above = lax.ppermute(up, "patch", [(p, p + 1) for p in range(patches - 1)])
    below = lax.ppermute(down, "patch", [(p + 1, p) for p in range(patches - 1)])
    second, third, last_image, sums = pl.pallas_call(
        krylov_kernel,
        out_shape=[shape(wide, LANES), shape(wide, LANES), shape(wide, LANES), shape(patches, SHARED)],
        in_specs=vmem(9), out_specs=vmem(4), scratch_shapes=scatter_scratch(3),
        compiler_params=params, name="krylov",
    )(whole, factors, hot_lane, hot_row, first, image, diagonal, above, below)
    sums = lax.all_to_all(sums, "patch", 0, 0, tiled=True)
    return pl.pallas_call(
        finish_kernel, out_shape=[shape(*positions.shape)] * 2,
        in_specs=vmem(6), out_specs=vmem(2), compiler_params=params, name="finish",
    )(sums, first, second, third, last_image, diagonal)


def solution(mesh):
    split = P(None, ("patch", "elem"))
    placed = (split,) * 5 + (P(("patch", "elem")),) + (P(),) * 4
    return jax.shard_map(per_device, mesh=mesh, in_specs=placed, out_specs=(split, split), check_vma=False)
```

```python
import functools

import jax
import jax.numpy as jnp
from jax import lax
from jax.experimental import pallas as pl
from jax.experimental.pallas import tpu as pltpu
from jax.sharding import PartitionSpec as P

STIFF = 1.0
REG = 0.1
GROUPS = 8
LANES = 128
TRI_CHUNKS = 6
VERT_CHUNKS = 2
ROWS = VERT_CHUNKS * GROUPS
TRI_ROWS = TRI_CHUNKS * GROUPS

POS, TGT, INERTIA, INC, RINV, RIM, COUNT, PACKED = 0, 6, 12, 14, 32, 56, 59, 64

HID1, HID2, LAST, WEIGHTS = 16, 144, 272, 368

QUANTA = 2.0**20 - 1.0
SHARED = 16

F32 = jnp.float32
BF16 = jnp.bfloat16


def vmem(n):
    return [pl.BlockSpec(memory_space=pltpu.VMEM)] * n


def iota(shape, axis):
    return lax.broadcasted_iota(jnp.int32, shape, axis)


def pack_kernel(pos, tgt, inertia, inc, rinv, w_in, w_hid1, w_hid2, w_out, out, weights):
    weights[0:16] = jnp.concatenate([w_in[...].astype(F32), jnp.zeros((10, LANES), F32)], axis=0).astype(BF16)
    weights[HID1:HID2] = w_hid1[...]
    weights[HID2:LAST] = w_hid2[...]
    weights[LAST:WEIGHTS] = jnp.concatenate([w_out[...].astype(F32), jnp.zeros((6, LANES), F32)], axis=0).astype(BF16)
    out[0] = jnp.zeros((PACKED, LANES), F32)
    for k in range(VERT_CHUNKS):
        cut = slice(k * LANES, (k + 1) * LANES)
        out[0, POS + 3 * k : POS + 3 * k + 3] = pos[:, cut]
        out[0, TGT + 3 * k : TGT + 3 * k + 3] = tgt[:, cut]
        out[0, INERTIA + k : INERTIA + k + 1] = inertia[:, cut]
    for k in range(TRI_CHUNKS):
        cut = slice(k * LANES, (k + 1) * LANES)
        out[0, INC + 3 * k : INC + 3 * k + 3] = inc[:, cut].astype(F32)
        out[0, RINV + 4 * k : RINV + 4 * k + 4] = rinv[:, cut]
    block = out[0]
    for e in range(1, GROUPS):
        out[e] = block


def rim_kernel(packed, rim, counts, out):
    del packed
    first = lax.axis_index("elem") == 0
    ends = jnp.where(first, rim[:, :LANES], rim[:, LANES:])
    count = jnp.full((1, LANES), counts[0], jnp.int32).astype(F32)
    tile = jnp.concatenate([ends, count, jnp.zeros((PACKED - COUNT - 1, LANES), F32)], axis=0)
    out[...] = jnp.broadcast_to(tile[None], out.shape)


def lane_rows(ref, row):
    return ref[pl.ds(row, GROUPS, stride=PACKED), :]


def corner_of(whole, k, q):
    index = lane_rows(whole, INC + 3 * k + q).astype(jnp.int32)
    row = ((index >> 7) & 1) * GROUPS + (index >> 8)
    return row, index & (LANES - 1)


def valid_of(whole, k):
    slot = iota((GROUPS, LANES), 1) + k * LANES
    return (slot.astype(F32) < lane_rows(whole, COUNT)).astype(F32)


def one_hot(row, lane, q, k, hot_lane, hot_row, stage):
    stage[0:8] = row.astype(F32)
    stage[8:16] = lane.astype(F32)
    places = iota((LANES, LANES), 0).astype(F32)
    for e in range(GROUPS):
        at = q * GROUPS * LANES + e * LANES
        for ref, first, count in ((hot_row, e, ROWS), (hot_lane, 8 + e, LANES)):
            line = jnp.broadcast_to(stage[first : first + 1, :], (count, LANES))
            ref[k, :, at : at + LANES] = jnp.where(line == places[:count], 1.0, 0.0).astype(BF16)


def gather(field, places):
    found = [[jnp.zeros((GROUPS, LANES), F32)] * 3 for _ in places]
    for h in range(ROWS):
        here = [row == h for row, _ in places]
        for c in range(3):
            line = jnp.broadcast_to(field[c * ROWS + h : c * ROWS + h + 1, :], (GROUPS, LANES))
            for q, (_, lane) in enumerate(places):
                value = jnp.take_along_axis(line, lane, axis=1, mode="promise_in_bounds")
                found[q][c] = jnp.where(here[q], value, found[q][c])
    return found


def quantized(field, words):
    top = jnp.max(jnp.max(jnp.abs(field[...]), axis=0, keepdims=True), axis=1, keepdims=True)
    step = jnp.maximum(top, 1e-32) / QUANTA
    x, y, z = [jnp.round(field[c * ROWS : (c + 1) * ROWS] * (1.0 / step)).astype(jnp.int32) for c in range(3)]
    words[0:ROWS] = (x << 11) | ((z >> 10) & 2047)
    words[ROWS : 2 * ROWS] = (y << 11) | (z & 1023)
    return step


def gather_words(words, step, places):
    found = [[jnp.zeros((GROUPS, LANES), jnp.int32)] * 2 for _ in places]
    for h in range(ROWS):
        here = [row == h for row, _ in places]
        for w in range(2):
            line = jnp.broadcast_to(words[w * ROWS + h : w * ROWS + h + 1, :], (GROUPS, LANES))
            for q, (_, lane) in enumerate(places):
                value = jnp.take_along_axis(line, lane, axis=1, mode="promise_in_bounds")
                found[q][w] = jnp.where(here[q], value, found[q][w])
    out = []
    for one, two in found:
        parts = (one >> 11, two >> 11, (((one << 21) >> 21) << 10) | (two & 1023))
        out.append([part.astype(F32) * step for part in parts])
    return out


def spread_out(values, k, hot_row, stage, spread):
    comps = len(values[0])
    for q in range(3):
        for c, value in enumerate(values[q]):
            upper = value.astype(BF16).astype(F32)
            stage[q, 8 * c : 8 * c + 8] = upper
            stage[q, 8 * (comps + c) : 8 * (comps + c) + 8] = value - upper
        for e in range(GROUPS):
            at = q * GROUPS * LANES + e * LANES
            mask = hot_row[k, :, at : at + LANES]
            for c in range(2 * comps):
                line = jnp.broadcast_to(stage[q, 8 * c + e : 8 * c + e + 1, :], (ROWS, LANES)).astype(BF16)
                spread[ROWS * c : ROWS * (c + 1), at : at + LANES] = line * mask


def collect(spread, k, hot_lane):
    return lax.dot_general(spread[...], hot_lane[k], (((1,), (1,)), ((), ())), preferred_element_type=F32)


def sweep(build, hot_lane, spreads, total):
    total[...] = jnp.zeros_like(total)
    for k in range(TRI_CHUNKS):
        if k > 0:
            total[...] += collect(spreads[(k - 1) % 2], k - 1, hot_lane)
        build(k, spreads[k % 2], k % 2)
    half = total.shape[0] // 2
    whole = total[...] + collect(spreads[(TRI_CHUNKS - 1) % 2], TRI_CHUNKS - 1, hot_lane)
    total[0:half] = whole[:half] + whole[half:]


def chain(here, before=None, after=None):
    lane = iota((GROUPS, LANES), 1)
    sub = iota((GROUPS, LANES), 0)
    low, high = here
    low_up, high_up = pltpu.roll(low, 1, 1), pltpu.roll(high, 1, 1)
    low_down, high_down = pltpu.roll(low, LANES - 1, 1), pltpu.roll(high, LANES - 1, 1)
    edge = 0.0 if before is None else pltpu.roll(jnp.broadcast_to(before, (GROUPS, LANES)), 1, 1)
    rim = jnp.where(sub == 0, edge, pltpu.roll(high_up, 1, 0))
    before_low = jnp.where(lane == 0, rim, low_up)
    before_high = jnp.where(lane == 0, low_up, high_up)
    edge = 0.0 if after is None else pltpu.roll(jnp.broadcast_to(after, (GROUPS, LANES)), LANES - 1, 1)
    rim = jnp.where(sub == GROUPS - 1, edge, pltpu.roll(low_down, GROUPS - 1, 0))
    after_low = jnp.where(lane == LANES - 1, high_down, low_down)
    after_high = jnp.where(lane == LANES - 1, rim, high_down)
    return (STIFF * (2.0 * low - before_low - after_low), STIFF * (2.0 * high - before_high - after_high))


def chunks(ref, c):
    at = c * ROWS
    return ref[at : at + GROUPS, :], ref[at + GROUPS : at + ROWS, :]


def put(ref, c, pair):
    at = c * ROWS
    ref[at : at + GROUPS, :] = pair[0]
    ref[at + GROUPS : at + ROWS, :] = pair[1]


def elements(whole, factors, hot_lane, hot_row, field, words, stage, spreads, total):
    step = quantized(field, words)

    def find(k):
        return gather_words(words, step, [corner_of(whole, k, q) for q in range(3)])

    ahead = [find(0)]

    def build(k, spread, turn):
        found = ahead.pop()
        u = found[0] + found[1] + found[2]
        if k + 1 < TRI_CHUNKS:
            ahead.append(find(k + 1))

        def factor(j, m):
            return factors[pl.ds(pl.multiple_of((9 * j + m) * TRI_ROWS + k * GROUPS, GROUPS), GROUPS), :]

        inner = [sum(factor(j, m) * u[j] for j in range(9)) * (1.0 / 9.0) for m in range(9)]
        shift = REG * valid_of(whole, k)
        out = [sum(factor(j, m) * inner[m] for m in range(9)) + shift * u[j] for j in range(9)]
        spread_out([out[0:3], out[3:6], out[6:9]], k, hot_row, stage.at[turn], spread)

    sweep(build, hot_lane, spreads, total)


def inertia_of(whole):
    return [lane_rows(whole, INERTIA + k) for k in range(VERT_CHUNKS)]


def apply_local(whole, factors, hots, field, words, stage, spreads, total, befores=None, afters=None):
    elements(whole, factors, *hots, field, words, stage, spreads, total)
    mass = inertia_of(whole)
    out = []
    for c in range(3):
        v = chunks(field, c)
        bent = chain(v, befores and befores[c], afters and afters[c])
        felt = chunks(total, c)
        out.append([mass[k] * v[k] + bent[k] + felt[k] for k in range(VERT_CHUNKS)])
    return out


def setup_kernel(whole, weights, factors, hot_lane, hot_row, first, image, diagonal, up, down,
                 pos, feats, inputs, outputs, raw, stage6, spread6a, spread6b, total6,
                 words, stage, spread_a, spread_b, total):
    for c in range(3):
        put(pos, c, [lane_rows(whole, POS + 3 * k + c) for k in range(VERT_CHUNKS)])
    feats[...] = jnp.zeros_like(feats)

    for k in range(TRI_CHUNKS):
        feat = feats.at[k % 2]
        places = [corner_of(whole, k, q) for q in range(3)]
        for q, (row, lane) in enumerate(places):
            one_hot(row, lane, q, k, hot_lane, hot_row, stage.at[k % 2, q])
        x0, x1, x2 = gather(pos, places)
        a, b, c_, d = [lane_rows(whole, RINV + 4 * k + i) for i in range(4)]
        for c in range(3):
            one, two = x1[c] - x0[c], x2[c] - x0[c]
            feat[pl.ds(c, GROUPS, stride=16), :] = one * a + two * c_
            feat[pl.ds(3 + c, GROUPS, stride=16), :] = one * b + two * d
        inputs[k] = jnp.concatenate([feat[16 * e : 16 * e + 16, :] for e in range(GROUPS)], axis=1).astype(BF16)

    x = jnp.concatenate([inputs[k] for k in range(TRI_CHUNKS)], axis=1)
    h = lax.dot_general(weights[0:HID1], x, (((0,), (0,)), ((), ())), preferred_element_type=F32)
    h = jnp.tanh(h).astype(BF16)
    for weight in (weights[HID1:HID2], weights[HID2:LAST]):
        h = jnp.tanh(jnp.dot(weight, h, preferred_element_type=F32)).astype(BF16)
    o = jnp.dot(weights[LAST:WEIGHTS], h, preferred_element_type=F32)
    for k in range(TRI_CHUNKS):
        outputs[k] = o[:, k * GROUPS * LANES : (k + 1) * GROUPS * LANES]

    def build(k, spread, turn):
        for e in range(GROUPS):
            for g in range(12):
                raw[pl.ds(g * 64 + e, 8, stride=8), :] = outputs[k, 8 * g : 8 * g + 8, e * LANES : (e + 1) * LANES]
        valid = valid_of(whole, k)
        forces, curves = [], []
        for j in range(9):
            forces.append(raw[8 * j : 8 * j + 8, :] * valid)
            curve = 0.0
            for m in range(9):
                at = 9 * j + m
                g = (raw[8 * (9 + at) : 8 * (9 + at) + 8, :] * valid).astype(BF16).astype(F32)
                factors[pl.ds(pl.multiple_of(at * TRI_ROWS + k * GROUPS, GROUPS), GROUPS), :] = g
                curve += g * g
            curves.append(curve * (1.0 / 9.0) + REG * valid)
        values = [forces[3 * q : 3 * q + 3] + curves[3 * q : 3 * q + 3] for q in range(3)]
        spread_out(values, k, hot_row, stage6.at[turn], spread)

    sweep(build, hot_lane, (spread6a, spread6b), total6)
    mass = inertia_of(whole)
    inverse = []
    for c in range(3):
        x = chunks(pos, c)
        bent = chain(x, whole[(GROUPS - 1) * PACKED + RIM + c : (GROUPS - 1) * PACKED + RIM + c + 1, :],
                     whole[RIM + c : RIM + c + 1, :])
        felt, curve = chunks(total6, c), chunks(total6, 3 + c)
        diag = [mass[k] + curve[k] + 2.0 * STIFF for k in range(VERT_CHUNKS)]
        inv = [1.0 / diag[k] for k in range(VERT_CHUNKS)]
        grad = [mass[k] * (x[k] - lane_rows(whole, TGT + 3 * k + c)) + bent[k] + felt[k]
                for k in range(VERT_CHUNKS)]
        put(diagonal, c, diag)
        put(first, c, [-grad[k] * inv[k] for k in range(VERT_CHUNKS)])
        inverse.append(inv)
    w = apply_local(whole, factors, (hot_lane, hot_row), first, words, stage, (spread_a, spread_b), total)
    up[...] = jnp.zeros_like(up)
    down[...] = jnp.zeros_like(down)
    for c in range(3):
        v = chunks(first, c)
        put(image, c, w[c])
        nxt = [w[c][k] * inverse[c][k] - v[k] for k in range(VERT_CHUNKS)]
        for i, what in enumerate((v, nxt, inverse[c])):
            up[3 * i + c : 3 * i + c + 1, :] = what[1][GROUPS - 1 : GROUPS, :]
            down[3 * i + c : 3 * i + c + 1, :] = what[0][0:1, :]


def krylov_kernel(whole, factors, hot_lane, hot_row, first, image, diagonal, above, below,
                  second, third, last_image, sums, words, stage, spread_a, spread_b, total):
    hots, spreads = (hot_lane, hot_row), (spread_a, spread_b)
    lane = iota((GROUPS, LANES), 1)
    sub = iota((GROUPS, LANES), 0)
    head = (lane == 0) & (sub == 0)
    tail = (lane == LANES - 1) & (sub == GROUPS - 1)

    def spread(row):
        return jnp.broadcast_to(row, (GROUPS, LANES))

    befores, afters = [], []
    for c in range(3):
        v0, w0 = chunks(first, c), chunks(image, c)
        diag = chunks(diagonal, c)
        inv = [1.0 / diag[k] for k in range(VERT_CHUNKS)]
        old_up, old_down = above[c : c + 1, :], below[c : c + 1, :]
        w_low = w0[0] - STIFF * jnp.where(head, pltpu.roll(spread(old_up), 1, 1), 0.0)
        w_high = w0[1] - STIFF * jnp.where(tail, pltpu.roll(spread(old_down), LANES - 1, 1), 0.0)
        put(second, c, [w_low * inv[0] - v0[0], w_high * inv[1] - v0[1]])
        mine_low = pltpu.roll(spread(v0[0][0:1, :]), LANES - 1, 1)[0:1, :]
        mine_high = pltpu.roll(spread(v0[1][GROUPS - 1 : GROUPS, :]), 1, 1)[0:1, :]
        befores.append(above[3 + c : 4 + c, :] - STIFF * mine_low * above[6 + c : 7 + c, :])
        afters.append(below[3 + c : 4 + c, :] - STIFF * mine_high * below[6 + c : 7 + c, :])
    w = apply_local(whole, factors, hots, second, words, stage, spreads, total, befores, afters)
    for c in range(3):
        diag, v1 = chunks(diagonal, c), chunks(second, c)
        put(third, c, [w[c][k] / diag[k] - v1[k] for k in range(VERT_CHUNKS)])
    w = apply_local(whole, factors, hots, third, words, stage, spreads, total)
    moment = [0.0] * 6
    ends = []
    for c in range(3):
        put(last_image, c, w[c])
        diag = chunks(diagonal, c)
        v0, v1, v2 = chunks(first, c), chunks(second, c), chunks(third, c)
        for k in range(VERT_CHUNKS):
            m0, m1, m2 = diag[k] * v0[k], diag[k] * v1[k], diag[k] * v2[k]
            for i, term in enumerate((m0 * v0[k], m0 * v1[k], m1 * v1[k], m1 * v2[k], m2 * v2[k],
                                      v2[k] * w[c][k] - m2 * v2[k])):
                moment[i] += term
        ends.append((jnp.where(head, v2[0], 0.0), jnp.where(tail, v2[1], 0.0)))
    line = jnp.zeros((1, LANES), F32)
    for i, part in enumerate(moment + [x[0] for x in ends] + [x[1] for x in ends]):
        value = jnp.sum(jnp.sum(part, axis=0, keepdims=True), axis=1, keepdims=True)
        line = jnp.where(iota((1, LANES), 1) == i, value, line)
    sums[...] = jnp.broadcast_to(line[:, 0:SHARED], sums.shape)


def finish_kernel(sums, first, second, third, last_image, diagonal, field, residual):
    patch, elem = lax.axis_index("patch"), lax.axis_index("elem")
    patches = sums.shape[0]
    every = sums[...]
    lane = iota(every.shape, 1)
    sub = iota(every.shape, 0)
    totals = jnp.sum(every, axis=0, keepdims=True)

    def pick(row, i):
        return row[:, i : i + 1]

    after = pltpu.roll(pltpu.roll(every, patches - 1, 0), 3, 1)
    coupled = jnp.where((lane >= 9) & (lane < 12) & (sub < patches - 1), every * after, 0.0)
    coupling = jnp.sum(jnp.sum(coupled, axis=0, keepdims=True), axis=1, keepdims=True)
    mu = [pick(totals, i) for i in range(6)]
    mu[5] = mu[5] - 2.0 * STIFF * coupling

    def inner(p, q):
        return sum(a * b * mu[i + j] for i, a in enumerate(p) for j, b in enumerate(q))

    def applied(p):
        padded = list(p) + [0.0 * mu[0]]
        return [padded[0]] + [padded[j] + padded[j - 1] for j in range(1, len(padded))]

    one = jnp.ones((1, 1), F32)
    z, direction, x = [one], [one], []
    rz = inner(z, z)
    for step in range(3):
        ahead = applied(direction)
        alpha = rz / inner(direction, ahead)
        x = [(x[j] if j < len(x) else 0.0) + alpha * direction[j] for j in range(len(direction))]
        z = [(z[j] if j < len(z) else 0.0) - alpha * ahead[j] for j in range(len(ahead))]
        if step < 2:
            new = inner(z, z)
            ratio = new / rz
            direction = [z[j] + (ratio * direction[j] if j < len(direction) else 0.0) for j in range(len(z))]
            rz = new
    place = iota((1, LANES), 1)
    prev = sums[pl.ds(jnp.maximum(patch - 1, 0), 1), :]
    nxt = sums[pl.ds(jnp.minimum(patch + 1, patches - 1), 1), :]
    at_head = (place == 0) & (elem == 0) & (patch > 0)
    at_tail = (place == LANES - 1) & (elem == GROUPS - 1) & (patch < patches - 1)
    for c in range(3):
        for k in range(VERT_CHUNKS):
            at = pl.ds(c * ROWS + k * GROUPS + elem, 1)
            v0, v1, v2, w2, diag = first[at, :], second[at, :], third[at, :], last_image[at, :], diagonal[at, :]
            if k == 0:
                w2 = w2 - STIFF * jnp.where(at_head, pick(prev, 9 + c), 0.0)
            else:
                w2 = w2 - STIFF * jnp.where(at_tail, pick(nxt, 6 + c), 0.0)
            v3 = w2 / diag - v2
            cut = slice(k * LANES, (k + 1) * LANES)
            field[c : c + 1, cut] = x[0] * v0 + x[1] * v1 + x[2] * v2
            residual[c : c + 1, cut] = diag * (z[0] * v0 + z[1] * v1 + z[2] * v2 + z[3] * v3)


def shape(*dims):
    return jax.ShapeDtypeStruct(dims, F32)


def per_device(positions, target, inertia, incidence, rest_inverse, counts, w_in, w_hid1, w_hid2, w_out):
    patches = lax.axis_size("patch")
    params = pltpu.CompilerParams(vmem_limit_bytes=16 * 1024 * 1024)
    moves = []
    for p in range(patches - 1):
        left, right = p * GROUPS, (p + 1) * GROUPS
        moves += [(left + GROUPS - 1, right + GROUPS - 1), (right, left)]
    rim = lax.ppermute(positions, ("patch", "elem"), moves)
    packed, weights = pl.pallas_call(
        pack_kernel, out_shape=[shape(GROUPS, PACKED, LANES), jax.ShapeDtypeStruct((WEIGHTS, LANES), BF16)],
        in_specs=vmem(9), out_specs=vmem(2), name="pack",
    )(positions, target, inertia, incidence, rest_inverse, w_in.T, w_hid1, w_hid2, w_out)
    packed = pl.pallas_call(
        rim_kernel, grid=(1,), out_shape=shape(GROUPS, PACKED, LANES),
        in_specs=[pl.BlockSpec(memory_space=pl.ANY)] + vmem(1) + [pl.BlockSpec(memory_space=pltpu.SMEM)],
        out_specs=pl.BlockSpec((GROUPS, PACKED - RIM, LANES), lambda i: (0, RIM // (PACKED - RIM), 0)),
        input_output_aliases={0: 0}, name="rim",
    )(packed, rim, counts)
    whole = lax.all_to_all(packed, "elem", 0, 0, tiled=True).reshape(GROUPS * PACKED, LANES)
    wide = 3 * ROWS
    width = GROUPS * LANES
    words = [pltpu.VMEM((2 * ROWS, LANES), jnp.int32)]

    def scatter_scratch(comps):
        spread = pltpu.VMEM((2 * comps * ROWS, 3 * width), BF16)
        return [pltpu.VMEM((2, 3, 2 * comps * GROUPS, LANES), F32), spread, spread,
                pltpu.VMEM((2 * comps * ROWS, LANES), F32)]

    factors, hot_lane, hot_row, first, image, diagonal, up, down = pl.pallas_call(
        setup_kernel,
        out_shape=[shape(81 * TRI_ROWS, LANES), jax.ShapeDtypeStruct((TRI_CHUNKS, LANES, 3 * width), BF16),
                   jax.ShapeDtypeStruct((TRI_CHUNKS, ROWS, 3 * width), BF16),
                   shape(wide, LANES), shape(wide, LANES), shape(wide, LANES), shape(16, LANES), shape(16, LANES)],
        in_specs=vmem(2), out_specs=vmem(8),
        scratch_shapes=[pltpu.VMEM((wide, LANES), F32), pltpu.VMEM((2, GROUPS * 16, LANES), F32),
                        pltpu.VMEM((TRI_CHUNKS, 16, width), BF16), pltpu.VMEM((TRI_CHUNKS, 96, width), F32),
                        pltpu.VMEM((96 * GROUPS, LANES), F32)] + scatter_scratch(6) + words + scatter_scratch(3),
        compiler_params=params, name="setup",
    )(whole, weights)
    above = lax.ppermute(up, "patch", [(p, p + 1) for p in range(patches - 1)])
    below = lax.ppermute(down, "patch", [(p + 1, p) for p in range(patches - 1)])
    second, third, last_image, sums = pl.pallas_call(
        krylov_kernel,
        out_shape=[shape(wide, LANES), shape(wide, LANES), shape(wide, LANES), shape(patches, SHARED)],
        in_specs=vmem(9), out_specs=vmem(4), scratch_shapes=words + scatter_scratch(3),
        compiler_params=params, name="krylov",
    )(whole, factors, hot_lane, hot_row, first, image, diagonal, above, below)
    sums = lax.all_to_all(sums, "patch", 0, 0, tiled=True)
    return pl.pallas_call(
        finish_kernel, out_shape=[shape(*positions.shape)] * 2,
        in_specs=vmem(6), out_specs=vmem(2), compiler_params=params, name="finish",
    )(sums, first, second, third, last_image, diagonal)


def solution(mesh):
    split = P(None, ("patch", "elem"))
    placed = (split,) * 5 + (P(("patch", "elem")),) + (P(),) * 4
    return jax.shard_map(per_device, mesh=mesh, in_specs=placed, out_specs=(split, split), check_vma=False)
```

```python
import functools

import jax
import jax.numpy as jnp
from jax import lax
from jax.experimental import pallas as pl
from jax.experimental.pallas import tpu as pltpu
from jax.sharding import PartitionSpec as P

STIFF = 1.0
REG = 0.1
GROUPS = 8
LANES = 128
TRI_CHUNKS = 6
VERT_CHUNKS = 2
ROWS = VERT_CHUNKS * GROUPS
TRI_ROWS = TRI_CHUNKS * GROUPS

POS, TGT, INERTIA, INC, RINV, RIM, COUNT, PACKED = 0, 6, 12, 14, 32, 56, 59, 64

HID1, HID2, LAST, WEIGHTS = 16, 144, 272, 368

QUANTA = 2.0**20 - 1.0
SHARED = 16

F32 = jnp.float32
BF16 = jnp.bfloat16


def vmem(n):
    return [pl.BlockSpec(memory_space=pltpu.VMEM)] * n


def iota(shape, axis):
    return lax.broadcasted_iota(jnp.int32, shape, axis)


def pack_kernel(pos, tgt, inertia, inc, rinv, w_in, w_hid1, w_hid2, w_out, out, weights):
    weights[0:16] = jnp.concatenate([w_in[...].astype(F32), jnp.zeros((10, LANES), F32)], axis=0).astype(BF16)
    weights[HID1:HID2] = w_hid1[...]
    weights[HID2:LAST] = w_hid2[...]
    weights[LAST:WEIGHTS] = jnp.concatenate([w_out[...].astype(F32), jnp.zeros((6, LANES), F32)], axis=0).astype(BF16)
    out[0] = jnp.zeros((PACKED, LANES), F32)
    for k in range(VERT_CHUNKS):
        cut = slice(k * LANES, (k + 1) * LANES)
        out[0, POS + 3 * k : POS + 3 * k + 3] = pos[:, cut]
        out[0, TGT + 3 * k : TGT + 3 * k + 3] = tgt[:, cut]
        out[0, INERTIA + k : INERTIA + k + 1] = inertia[:, cut]
    for k in range(TRI_CHUNKS):
        cut = slice(k * LANES, (k + 1) * LANES)
        out[0, INC + 3 * k : INC + 3 * k + 3] = inc[:, cut].astype(F32)
        out[0, RINV + 4 * k : RINV + 4 * k + 4] = rinv[:, cut]
    block = out[0]
    for e in range(1, GROUPS):
        out[e] = block


def rim_kernel(packed, rim, counts, out):
    del packed
    first = lax.axis_index("elem") == 0
    ends = jnp.where(first, rim[:, :LANES], rim[:, LANES:])
    count = jnp.full((1, LANES), counts[0], jnp.int32).astype(F32)
    tile = jnp.concatenate([ends, count, jnp.zeros((PACKED - COUNT - 1, LANES), F32)], axis=0)
    out[...] = jnp.broadcast_to(tile[None], out.shape)


def lane_rows(ref, row):
    return ref[pl.ds(row, GROUPS, stride=PACKED), :]


def corner_of(whole, k, q):
    index = lane_rows(whole, INC + 3 * k + q).astype(jnp.int32)
    row = ((index >> 7) & 1) * GROUPS + (index >> 8)
    return row, index & (LANES - 1)


def valid_of(whole, k):
    slot = iota((GROUPS, LANES), 1) + k * LANES
    return (slot.astype(F32) < lane_rows(whole, COUNT)).astype(F32)


def one_hot(row, lane, q, k, hot_lane, hot_row, stage):
    stage[0:8] = row.astype(F32)
    stage[8:16] = lane.astype(F32)
    places = iota((LANES, LANES), 0).astype(F32)
    for e in range(GROUPS):
        at = q * GROUPS * LANES + e * LANES
        for ref, first, count in ((hot_row, e, ROWS), (hot_lane, 8 + e, LANES)):
            line = jnp.broadcast_to(stage[first : first + 1, :], (count, LANES))
            ref[k, :, at : at + LANES] = jnp.where(line == places[:count], 1.0, 0.0).astype(BF16)


def gather(field, places):
    found = [[jnp.zeros((GROUPS, LANES), F32)] * 3 for _ in places]
    for h in range(ROWS):
        here = [row == h for row, _ in places]
        for c in range(3):
            line = jnp.broadcast_to(field[c * ROWS + h : c * ROWS + h + 1, :], (GROUPS, LANES))
            for q, (_, lane) in enumerate(places):
                value = jnp.take_along_axis(line, lane, axis=1, mode="promise_in_bounds")
                found[q][c] = jnp.where(here[q], value, found[q][c])
    return found


def quantized(field, words):
    top = jnp.max(jnp.max(jnp.abs(field[...]), axis=0, keepdims=True), axis=1, keepdims=True)
    step = jnp.maximum(top, 1e-32) / QUANTA
    x, y, z = [jnp.round(field[c * ROWS : (c + 1) * ROWS] * (1.0 / step)).astype(jnp.int32) for c in range(3)]
    words[0:ROWS] = (x << 11) | ((z >> 10) & 2047)
    words[ROWS : 2 * ROWS] = (y << 11) | (z & 1023)
    return step


def gather_words(words, step, places):
    found = [[jnp.zeros((GROUPS, LANES), jnp.int32)] * 2 for _ in places]
    for h in range(ROWS):
        here = [row == h for row, _ in places]
        for w in range(2):
            line = jnp.broadcast_to(words[w * ROWS + h : w * ROWS + h + 1, :], (GROUPS, LANES))
            for q, (_, lane) in enumerate(places):
                value = jnp.take_along_axis(line, lane, axis=1, mode="promise_in_bounds")
                found[q][w] = jnp.where(here[q], value, found[q][w])
    out = []
    for one, two in found:
        parts = (one >> 11, two >> 11, (((one << 21) >> 21) << 10) | (two & 1023))
        out.append([part.astype(F32) * step for part in parts])
    return out


def spread_out(values, k, hot_row, stage, spread):
    comps = len(values[0])
    for q in range(3):
        for c, value in enumerate(values[q]):
            upper = value.astype(BF16).astype(F32)
            stage[q, 8 * c : 8 * c + 8] = upper
            stage[q, 8 * (comps + c) : 8 * (comps + c) + 8] = value - upper
        for e in range(GROUPS):
            at = q * GROUPS * LANES + e * LANES
            mask = hot_row[k, :, at : at + LANES]
            for c in range(2 * comps):
                line = jnp.broadcast_to(stage[q, 8 * c + e : 8 * c + e + 1, :], (ROWS, LANES)).astype(BF16)
                spread[ROWS * c : ROWS * (c + 1), at : at + LANES] = line * mask


def collect(spread, k, hot_lane):
    return lax.dot_general(spread[...], hot_lane[k], (((1,), (1,)), ((), ())), preferred_element_type=F32)


def sweep(build, hot_lane, spreads, total):
    total[...] = jnp.zeros_like(total)
    for k in range(TRI_CHUNKS):
        if k > 0:
            total[...] += collect(spreads[(k - 1) % 2], k - 1, hot_lane)
        build(k, spreads[k % 2], k % 2)
    half = total.shape[0] // 2
    whole = total[...] + collect(spreads[(TRI_CHUNKS - 1) % 2], TRI_CHUNKS - 1, hot_lane)
    total[0:half] = whole[:half] + whole[half:]


def chain(here, before=None, after=None):
    lane = iota((GROUPS, LANES), 1)
    sub = iota((GROUPS, LANES), 0)
    low, high = here
    low_up, high_up = pltpu.roll(low, 1, 1), pltpu.roll(high, 1, 1)
    low_down, high_down = pltpu.roll(low, LANES - 1, 1), pltpu.roll(high, LANES - 1, 1)
    edge = 0.0 if before is None else pltpu.roll(jnp.broadcast_to(before, (GROUPS, LANES)), 1, 1)
    rim = jnp.where(sub == 0, edge, pltpu.roll(high_up, 1, 0))
    before_low = jnp.where(lane == 0, rim, low_up)
    before_high = jnp.where(lane == 0, low_up, high_up)
    edge = 0.0 if after is None else pltpu.roll(jnp.broadcast_to(after, (GROUPS, LANES)), LANES - 1, 1)
    rim = jnp.where(sub == GROUPS - 1, edge, pltpu.roll(low_down, GROUPS - 1, 0))
    after_low = jnp.where(lane == LANES - 1, high_down, low_down)
    after_high = jnp.where(lane == LANES - 1, rim, high_down)
    return (STIFF * (2.0 * low - before_low - after_low), STIFF * (2.0 * high - before_high - after_high))


def chunks(ref, c):
    at = c * ROWS
    return ref[at : at + GROUPS, :], ref[at + GROUPS : at + ROWS, :]


def put(ref, c, pair):
    at = c * ROWS
    ref[at : at + GROUPS, :] = pair[0]
    ref[at + GROUPS : at + ROWS, :] = pair[1]


def elements(whole, factors, hot_lane, hot_row, field, words, stage, spreads, total):
    step = quantized(field, words)

    def find(k):
        return gather_words(words, step, [corner_of(whole, k, q) for q in range(3)])

    ahead = [find(0)]

    def build(k, spread, turn):
        found = ahead.pop()
        u = found[0] + found[1] + found[2]
        if k + 1 < TRI_CHUNKS:
            ahead.append(find(k + 1))

        def factor(j, m):
            return factors[pl.ds(pl.multiple_of((9 * j + m) * TRI_ROWS + k * GROUPS, GROUPS), GROUPS), :]

        inner = [sum(factor(j, m) * u[j] for j in range(9)) * (1.0 / 9.0) for m in range(9)]
        shift = REG * valid_of(whole, k)
        out = [sum(factor(j, m) * inner[m] for m in range(9)) + shift * u[j] for j in range(9)]
        spread_out([out[0:3], out[3:6], out[6:9]], k, hot_row, stage.at[turn], spread)

    sweep(build, hot_lane, spreads, total)


def inertia_of(whole):
    return [lane_rows(whole, INERTIA + k) for k in range(VERT_CHUNKS)]


def apply_local(whole, factors, hots, field, words, stage, spreads, total, befores=None, afters=None):
    elements(whole, factors, *hots, field, words, stage, spreads, total)
    mass = inertia_of(whole)
    out = []
    for c in range(3):
        v = chunks(field, c)
        bent = chain(v, befores and befores[c], afters and afters[c])
        felt = chunks(total, c)
        out.append([mass[k] * v[k] + bent[k] + felt[k] for k in range(VERT_CHUNKS)])
    return out


def setup_kernel(whole, weights, factors, hot_lane, hot_row, first, image, diagonal, up, down,
                 pos, feats, inputs, outputs, raw, stage6, spread6a, spread6b, total6,
                 words, stage, spread_a, spread_b, total):
    for c in range(3):
        put(pos, c, [lane_rows(whole, POS + 3 * k + c) for k in range(VERT_CHUNKS)])
    feats[...] = jnp.zeros_like(feats)

    for k in range(TRI_CHUNKS):
        feat = feats.at[k % 2]
        places = [corner_of(whole, k, q) for q in range(3)]
        for q, (row, lane) in enumerate(places):
            one_hot(row, lane, q, k, hot_lane, hot_row, stage.at[k % 2, q])
        x0, x1, x2 = gather(pos, places)
        a, b, c_, d = [lane_rows(whole, RINV + 4 * k + i) for i in range(4)]
        for c in range(3):
            one, two = x1[c] - x0[c], x2[c] - x0[c]
            feat[pl.ds(c, GROUPS, stride=16), :] = one * a + two * c_
            feat[pl.ds(3 + c, GROUPS, stride=16), :] = one * b + two * d
        inputs[k] = jnp.concatenate([feat[16 * e : 16 * e + 16, :] for e in range(GROUPS)], axis=1).astype(BF16)

    x = jnp.concatenate([inputs[k] for k in range(TRI_CHUNKS)], axis=1)
    h = lax.dot_general(weights[0:HID1], x, (((0,), (0,)), ((), ())), preferred_element_type=F32)
    h = jnp.tanh(h).astype(BF16)
    for weight in (weights[HID1:HID2], weights[HID2:LAST]):
        h = jnp.tanh(jnp.dot(weight, h, preferred_element_type=F32)).astype(BF16)
    o = jnp.dot(weights[LAST:WEIGHTS], h, preferred_element_type=F32)
    for k in range(TRI_CHUNKS):
        outputs[k] = o[:, k * GROUPS * LANES : (k + 1) * GROUPS * LANES]

    def build(k, spread, turn):
        for e in range(GROUPS):
            for g in range(12):
                raw[pl.ds(g * 64 + e, 8, stride=8), :] = outputs[k, 8 * g : 8 * g + 8, e * LANES : (e + 1) * LANES]
        valid = valid_of(whole, k)
        forces, curves = [], []
        for j in range(9):
            forces.append(raw[8 * j : 8 * j + 8, :] * valid)
            curve = 0.0
            for m in range(9):
                at = 9 * j + m
                g = (raw[8 * (9 + at) : 8 * (9 + at) + 8, :] * valid).astype(BF16).astype(F32)
                factors[pl.ds(pl.multiple_of(at * TRI_ROWS + k * GROUPS, GROUPS), GROUPS), :] = g
                curve += g * g
            curves.append(curve * (1.0 / 9.0) + REG * valid)
        values = [forces[3 * q : 3 * q + 3] + curves[3 * q : 3 * q + 3] for q in range(3)]
        spread_out(values, k, hot_row, stage6.at[turn], spread)

    sweep(build, hot_lane, (spread6a, spread6b), total6)
    mass = inertia_of(whole)
    inverse = []
    for c in range(3):
        x = chunks(pos, c)
        bent = chain(x, whole[(GROUPS - 1) * PACKED + RIM + c : (GROUPS - 1) * PACKED + RIM + c + 1, :],
                     whole[RIM + c : RIM + c + 1, :])
        felt, curve = chunks(total6, c), chunks(total6, 3 + c)
        diag = [mass[k] + curve[k] + 2.0 * STIFF for k in range(VERT_CHUNKS)]
        inv = [1.0 / diag[k] for k in range(VERT_CHUNKS)]
        grad = [mass[k] * (x[k] - lane_rows(whole, TGT + 3 * k + c)) + bent[k] + felt[k]
                for k in range(VERT_CHUNKS)]
        put(diagonal, c, diag)
        put(first, c, [-grad[k] * inv[k] for k in range(VERT_CHUNKS)])
        inverse.append(inv)
    w = apply_local(whole, factors, (hot_lane, hot_row), first, words, stage, (spread_a, spread_b), total)
    up[...] = jnp.zeros_like(up)
    down[...] = jnp.zeros_like(down)
    for c in range(3):
        v = chunks(first, c)
        put(image, c, w[c])
        nxt = [w[c][k] * inverse[c][k] - v[k] for k in range(VERT_CHUNKS)]
        for i, what in enumerate((v, nxt, inverse[c])):
            up[3 * i + c : 3 * i + c + 1, :] = what[1][GROUPS - 1 : GROUPS, :]
            down[3 * i + c : 3 * i + c + 1, :] = what[0][0:1, :]


def krylov_kernel(whole, factors, hot_lane, hot_row, first, image, diagonal, above, below,
                  second, third, last_image, sums, words, stage, spread_a, spread_b, total):
    hots, spreads = (hot_lane, hot_row), (spread_a, spread_b)
    lane = iota((GROUPS, LANES), 1)
    sub = iota((GROUPS, LANES), 0)
    head = (lane == 0) & (sub == 0)
    tail = (lane == LANES - 1) & (sub == GROUPS - 1)

    def spread(row):
        return jnp.broadcast_to(row, (GROUPS, LANES))

    befores, afters = [], []
    for c in range(3):
        v0, w0 = chunks(first, c), chunks(image, c)
        diag = chunks(diagonal, c)
        inv = [1.0 / diag[k] for k in range(VERT_CHUNKS)]
        old_up, old_down = above[c : c + 1, :], below[c : c + 1, :]
        w_low = w0[0] - STIFF * jnp.where(head, pltpu.roll(spread(old_up), 1, 1), 0.0)
        w_high = w0[1] - STIFF * jnp.where(tail, pltpu.roll(spread(old_down), LANES - 1, 1), 0.0)
        put(second, c, [w_low * inv[0] - v0[0], w_high * inv[1] - v0[1]])
        mine_low = pltpu.roll(spread(v0[0][0:1, :]), LANES - 1, 1)[0:1, :]
        mine_high = pltpu.roll(spread(v0[1][GROUPS - 1 : GROUPS, :]), 1, 1)[0:1, :]
        befores.append(above[3 + c : 4 + c, :] - STIFF * mine_low * above[6 + c : 7 + c, :])
        afters.append(below[3 + c : 4 + c, :] - STIFF * mine_high * below[6 + c : 7 + c, :])
    w = apply_local(whole, factors, hots, second, words, stage, spreads, total, befores, afters)
    for c in range(3):
        diag, v1 = chunks(diagonal, c), chunks(second, c)
        put(third, c, [w[c][k] / diag[k] - v1[k] for k in range(VERT_CHUNKS)])
    w = apply_local(whole, factors, hots, third, words, stage, spreads, total)
    moment = [0.0] * 6
    ends = []
    for c in range(3):
        put(last_image, c, w[c])
        diag = chunks(diagonal, c)
        v0, v1, v2 = chunks(first, c), chunks(second, c), chunks(third, c)
        for k in range(VERT_CHUNKS):
            m0, m1, m2 = diag[k] * v0[k], diag[k] * v1[k], diag[k] * v2[k]
            for i, term in enumerate((m0 * v0[k], m0 * v1[k], m1 * v1[k], m1 * v2[k], m2 * v2[k],
                                      v2[k] * w[c][k] - m2 * v2[k])):
                moment[i] += term
        ends.append((jnp.where(head, v2[0], 0.0), jnp.where(tail, v2[1], 0.0)))
    line = jnp.zeros((1, LANES), F32)
    for i, part in enumerate(moment + [x[0] for x in ends] + [x[1] for x in ends]):
        value = jnp.sum(jnp.sum(part, axis=0, keepdims=True), axis=1, keepdims=True)
        line = jnp.where(iota((1, LANES), 1) == i, value, line)
    sums[...] = jnp.broadcast_to(line[:, 0:SHARED], sums.shape)


def finish_kernel(sums, first, second, third, last_image, diagonal, field, residual):
    patch, elem = lax.axis_index("patch"), lax.axis_index("elem")
    patches = sums.shape[0]
    every = sums[...]
    lane = iota(every.shape, 1)
    sub = iota(every.shape, 0)
    totals = jnp.sum(every, axis=0, keepdims=True)

    def pick(row, i):
        return row[:, i : i + 1]

    after = pltpu.roll(pltpu.roll(every, patches - 1, 0), 3, 1)
    coupled = jnp.where((lane >= 9) & (lane < 12) & (sub < patches - 1), every * after, 0.0)
    coupling = jnp.sum(jnp.sum(coupled, axis=0, keepdims=True), axis=1, keepdims=True)
    mu = [pick(totals, i) for i in range(6)]
    mu[5] = mu[5] - 2.0 * STIFF * coupling

    def inner(p, q):
        return sum(a * b * mu[i + j] for i, a in enumerate(p) for j, b in enumerate(q))

    def applied(p):
        padded = list(p) + [0.0 * mu[0]]
        return [padded[0]] + [padded[j] + padded[j - 1] for j in range(1, len(padded))]

    one = jnp.ones((1, 1), F32)
    z, direction, x = [one], [one], []
    rz = inner(z, z)
    for step in range(3):
        ahead = applied(direction)
        alpha = rz / inner(direction, ahead)
        x = [(x[j] if j < len(x) else 0.0) + alpha * direction[j] for j in range(len(direction))]
        z = [(z[j] if j < len(z) else 0.0) - alpha * ahead[j] for j in range(len(ahead))]
        if step < 2:
            new = inner(z, z)
            ratio = new / rz
            direction = [z[j] + (ratio * direction[j] if j < len(direction) else 0.0) for j in range(len(z))]
            rz = new
    place = iota((1, LANES), 1)
    prev = sums[pl.ds(jnp.maximum(patch - 1, 0), 1), :]
    nxt = sums[pl.ds(jnp.minimum(patch + 1, patches - 1), 1), :]
    at_head = (place == 0) & (elem == 0) & (patch > 0)
    at_tail = (place == LANES - 1) & (elem == GROUPS - 1) & (patch < patches - 1)
    for c in range(3):
        for k in range(VERT_CHUNKS):
            at = pl.ds(c * ROWS + k * GROUPS + elem, 1)
            v0, v1, v2, w2, diag = first[at, :], second[at, :], third[at, :], last_image[at, :], diagonal[at, :]
            if k == 0:
                w2 = w2 - STIFF * jnp.where(at_head, pick(prev, 9 + c), 0.0)
            else:
                w2 = w2 - STIFF * jnp.where(at_tail, pick(nxt, 6 + c), 0.0)
            v3 = w2 / diag - v2
            cut = slice(k * LANES, (k + 1) * LANES)
            field[c : c + 1, cut] = x[0] * v0 + x[1] * v1 + x[2] * v2
            residual[c : c + 1, cut] = diag * (z[0] * v0 + z[1] * v1 + z[2] * v2 + z[3] * v3)


def shape(*dims):
    return jax.ShapeDtypeStruct(dims, F32)


def per_device(positions, target, inertia, incidence, rest_inverse, counts, w_in, w_hid1, w_hid2, w_out):
    patches = lax.axis_size("patch")
    params = pltpu.CompilerParams(vmem_limit_bytes=20 * 1024 * 1024)
    moves = []
    for p in range(patches - 1):
        left, right = p * GROUPS, (p + 1) * GROUPS
        moves += [(left + GROUPS - 1, right + GROUPS - 1), (right, left)]
    rim = lax.ppermute(positions, ("patch", "elem"), moves)
    packed, weights = pl.pallas_call(
        pack_kernel, out_shape=[shape(GROUPS, PACKED, LANES), jax.ShapeDtypeStruct((WEIGHTS, LANES), BF16)],
        in_specs=vmem(9), out_specs=vmem(2), name="pack",
    )(positions, target, inertia, incidence, rest_inverse, w_in.T, w_hid1, w_hid2, w_out)
    packed = pl.pallas_call(
        rim_kernel, grid=(1,), out_shape=shape(GROUPS, PACKED, LANES),
        in_specs=[pl.BlockSpec(memory_space=pl.ANY)] + vmem(1) + [pl.BlockSpec(memory_space=pltpu.SMEM)],
        out_specs=pl.BlockSpec((GROUPS, PACKED - RIM, LANES), lambda i: (0, RIM // (PACKED - RIM), 0)),
        input_output_aliases={0: 0}, compiler_params=params, name="rim",
    )(packed, rim, counts)
    whole = lax.all_to_all(packed, "elem", 0, 0, tiled=True).reshape(GROUPS * PACKED, LANES)
    wide = 3 * ROWS
    width = GROUPS * LANES
    words = [pltpu.VMEM((2 * ROWS, LANES), jnp.int32)]

    def scatter_scratch(comps):
        spread = pltpu.VMEM((2 * comps * ROWS, 3 * width), BF16)
        return [pltpu.VMEM((2, 3, 2 * comps * GROUPS, LANES), F32), spread, spread,
                pltpu.VMEM((2 * comps * ROWS, LANES), F32)]

    factors, hot_lane, hot_row, first, image, diagonal, up, down = pl.pallas_call(
        setup_kernel,
        out_shape=[shape(81 * TRI_ROWS, LANES), jax.ShapeDtypeStruct((TRI_CHUNKS, LANES, 3 * width), BF16),
                   jax.ShapeDtypeStruct((TRI_CHUNKS, ROWS, 3 * width), BF16),
                   shape(wide, LANES), shape(wide, LANES), shape(wide, LANES), shape(16, LANES), shape(16, LANES)],
        in_specs=vmem(2), out_specs=vmem(8),
        scratch_shapes=[pltpu.VMEM((wide, LANES), F32), pltpu.VMEM((2, GROUPS * 16, LANES), F32),
                        pltpu.VMEM((TRI_CHUNKS, 16, width), BF16), pltpu.VMEM((TRI_CHUNKS, 96, width), F32),
                        pltpu.VMEM((96 * GROUPS, LANES), F32)] + scatter_scratch(6) + words + scatter_scratch(3),
        compiler_params=params, name="setup",
    )(whole, weights)
    above = lax.ppermute(up, "patch", [(p, p + 1) for p in range(patches - 1)])
    below = lax.ppermute(down, "patch", [(p + 1, p) for p in range(patches - 1)])
    second, third, last_image, sums = pl.pallas_call(
        krylov_kernel,
        out_shape=[shape(wide, LANES), shape(wide, LANES), shape(wide, LANES), shape(patches, SHARED)],
        in_specs=vmem(9), out_specs=vmem(4), scratch_shapes=words + scatter_scratch(3),
        compiler_params=params, name="krylov",
    )(whole, factors, hot_lane, hot_row, first, image, diagonal, above, below)
    sums = lax.all_to_all(sums, "patch", 0, 0, tiled=True)
    return pl.pallas_call(
        finish_kernel, out_shape=[shape(*positions.shape)] * 2,
        in_specs=vmem(6), out_specs=vmem(2), compiler_params=params, name="finish",
    )(sums, first, second, third, last_image, diagonal)


def solution(mesh):
    split = P(None, ("patch", "elem"))
    placed = (split,) * 5 + (P(("patch", "elem")),) + (P(),) * 4
    return jax.shard_map(per_device, mesh=mesh, in_specs=placed, out_specs=(split, split), check_vma=False)
```

```python
import functools

import jax
import jax.numpy as jnp
from jax import lax
from jax.experimental import pallas as pl
from jax.experimental.pallas import tpu as pltpu
from jax.sharding import PartitionSpec as P

STIFF = 1.0
REG = 0.1
GROUPS = 8
LANES = 128
TRI_CHUNKS = 6
VERT_CHUNKS = 2
ROWS = VERT_CHUNKS * GROUPS
TRI_ROWS = TRI_CHUNKS * GROUPS

POS, TGT, INERTIA, INC, RINV, RIM, COUNT, PACKED = 0, 6, 12, 14, 32, 56, 59, 64

HID1, HID2, LAST, WEIGHTS = 16, 144, 272, 368

QUANTA = 2.0**20 - 1.0
SHARED = 16

F32 = jnp.float32
BF16 = jnp.bfloat16


def vmem(n):
    return [pl.BlockSpec(memory_space=pltpu.VMEM)] * n


def iota(shape, axis):
    return lax.broadcasted_iota(jnp.int32, shape, axis)


def pack_kernel(pos, tgt, inertia, inc, rinv, w_in, w_hid1, w_hid2, w_out, out, weights):
    weights[0:16] = jnp.concatenate([w_in[...].astype(F32), jnp.zeros((10, LANES), F32)], axis=0).astype(BF16)
    weights[HID1:HID2] = w_hid1[...]
    weights[HID2:LAST] = w_hid2[...]
    weights[LAST:WEIGHTS] = jnp.concatenate([w_out[...].astype(F32), jnp.zeros((6, LANES), F32)], axis=0).astype(BF16)
    out[0] = jnp.zeros((PACKED, LANES), F32)
    for k in range(VERT_CHUNKS):
        cut = slice(k * LANES, (k + 1) * LANES)
        out[0, POS + 3 * k : POS + 3 * k + 3] = pos[:, cut]
        out[0, TGT + 3 * k : TGT + 3 * k + 3] = tgt[:, cut]
        out[0, INERTIA + k : INERTIA + k + 1] = inertia[:, cut]
    for k in range(TRI_CHUNKS):
        cut = slice(k * LANES, (k + 1) * LANES)
        out[0, INC + 3 * k : INC + 3 * k + 3] = inc[:, cut].astype(F32)
        out[0, RINV + 4 * k : RINV + 4 * k + 4] = rinv[:, cut]
    block = out[0]
    for e in range(1, GROUPS):
        out[e] = block


def rim_kernel(packed, rim, counts, weights, out, weights_out):
    del packed, weights, weights_out
    first = lax.axis_index("elem") == 0
    ends = jnp.where(first, rim[:, :LANES], rim[:, LANES:])
    count = jnp.full((1, LANES), counts[0], jnp.int32).astype(F32)
    tile = jnp.concatenate([ends, count, jnp.zeros((PACKED - COUNT - 1, LANES), F32)], axis=0)
    out[...] = jnp.broadcast_to(tile[None], out.shape)


def lane_rows(ref, row):
    return ref[pl.ds(row, GROUPS, stride=PACKED), :]


def corner_of(whole, k, q):
    index = lane_rows(whole, INC + 3 * k + q).astype(jnp.int32)
    row = ((index >> 7) & 1) * GROUPS + (index >> 8)
    return row, index & (LANES - 1)


def valid_of(whole, k):
    slot = iota((GROUPS, LANES), 1) + k * LANES
    return (slot.astype(F32) < lane_rows(whole, COUNT)).astype(F32)


def one_hot(row, lane, q, k, hot_lane, hot_row, stage):
    stage[0:8] = row.astype(F32)
    stage[8:16] = lane.astype(F32)
    places = iota((LANES, LANES), 0).astype(F32)
    for e in range(GROUPS):
        at = q * GROUPS * LANES + e * LANES
        for ref, first, count in ((hot_row, e, ROWS), (hot_lane, 8 + e, LANES)):
            line = jnp.broadcast_to(stage[first : first + 1, :], (count, LANES))
            ref[k, :, at : at + LANES] = jnp.where(line == places[:count], 1.0, 0.0).astype(BF16)


def gather(field, places):
    found = [[jnp.zeros((GROUPS, LANES), F32)] * 3 for _ in places]
    for h in range(ROWS):
        here = [row == h for row, _ in places]
        for c in range(3):
            line = jnp.broadcast_to(field[c * ROWS + h : c * ROWS + h + 1, :], (GROUPS, LANES))
            for q, (_, lane) in enumerate(places):
                value = jnp.take_along_axis(line, lane, axis=1, mode="promise_in_bounds")
                found[q][c] = jnp.where(here[q], value, found[q][c])
    return found


def quantized(field, words):
    top = jnp.max(jnp.max(jnp.abs(field[...]), axis=0, keepdims=True), axis=1, keepdims=True)
    step = jnp.maximum(top, 1e-32) / QUANTA
    x, y, z = [jnp.round(field[c * ROWS : (c + 1) * ROWS] * (1.0 / step)).astype(jnp.int32) for c in range(3)]
    words[0:ROWS] = (x << 11) | ((z >> 10) & 2047)
    words[ROWS : 2 * ROWS] = (y << 11) | (z & 1023)
    return step


def gather_words(words, step, places):
    found = [[jnp.zeros((GROUPS, LANES), jnp.int32)] * 2 for _ in places]
    for h in range(ROWS):
        here = [row == h for row, _ in places]
        for w in range(2):
            line = jnp.broadcast_to(words[w * ROWS + h : w * ROWS + h + 1, :], (GROUPS, LANES))
            for q, (_, lane) in enumerate(places):
                value = jnp.take_along_axis(line, lane, axis=1, mode="promise_in_bounds")
                found[q][w] = jnp.where(here[q], value, found[q][w])
    out = []
    for one, two in found:
        parts = (one >> 11, two >> 11, (((one << 21) >> 21) << 10) | (two & 1023))
        out.append([part.astype(F32) * step for part in parts])
    return out


def spread_out(values, k, hot_row, stage, spread):
    comps = len(values[0])
    for q in range(3):
        for c, value in enumerate(values[q]):
            upper = value.astype(BF16).astype(F32)
            stage[q, 8 * c : 8 * c + 8] = upper
            stage[q, 8 * (comps + c) : 8 * (comps + c) + 8] = value - upper
        for e in range(GROUPS):
            at = q * GROUPS * LANES + e * LANES
            mask = hot_row[k, :, at : at + LANES]
            for c in range(2 * comps):
                line = jnp.broadcast_to(stage[q, 8 * c + e : 8 * c + e + 1, :], (ROWS, LANES)).astype(BF16)
                spread[ROWS * c : ROWS * (c + 1), at : at + LANES] = line * mask


def collect(spread, k, hot_lane):
    return lax.dot_general(spread[...], hot_lane[k], (((1,), (1,)), ((), ())), preferred_element_type=F32)


def sweep(build, hot_lane, spreads, total):
    total[...] = jnp.zeros_like(total)
    for k in range(TRI_CHUNKS):
        if k > 0:
            total[...] += collect(spreads[(k - 1) % 2], k - 1, hot_lane)
        build(k, spreads[k % 2], k % 2)
    half = total.shape[0] // 2
    whole = total[...] + collect(spreads[(TRI_CHUNKS - 1) % 2], TRI_CHUNKS - 1, hot_lane)
    total[0:half] = whole[:half] + whole[half:]


def chain(here, before=None, after=None):
    lane = iota((GROUPS, LANES), 1)
    sub = iota((GROUPS, LANES), 0)
    low, high = here
    low_up, high_up = pltpu.roll(low, 1, 1), pltpu.roll(high, 1, 1)
    low_down, high_down = pltpu.roll(low, LANES - 1, 1), pltpu.roll(high, LANES - 1, 1)
    edge = 0.0 if before is None else pltpu.roll(jnp.broadcast_to(before, (GROUPS, LANES)), 1, 1)
    rim = jnp.where(sub == 0, edge, pltpu.roll(high_up, 1, 0))
    before_low = jnp.where(lane == 0, rim, low_up)
    before_high = jnp.where(lane == 0, low_up, high_up)
    edge = 0.0 if after is None else pltpu.roll(jnp.broadcast_to(after, (GROUPS, LANES)), LANES - 1, 1)
    rim = jnp.where(sub == GROUPS - 1, edge, pltpu.roll(low_down, GROUPS - 1, 0))
    after_low = jnp.where(lane == LANES - 1, high_down, low_down)
    after_high = jnp.where(lane == LANES - 1, rim, high_down)
    return (STIFF * (2.0 * low - before_low - after_low), STIFF * (2.0 * high - before_high - after_high))


def chunks(ref, c):
    at = c * ROWS
    return ref[at : at + GROUPS, :], ref[at + GROUPS : at + ROWS, :]


def put(ref, c, pair):
    at = c * ROWS
    ref[at : at + GROUPS, :] = pair[0]
    ref[at + GROUPS : at + ROWS, :] = pair[1]


def elements(whole, factors, hot_lane, hot_row, field, words, stage, spreads, total):
    step = quantized(field, words)

    def find(k):
        return gather_words(words, step, [corner_of(whole, k, q) for q in range(3)])

    ahead = [find(0)]

    def build(k, spread, turn):
        found = ahead.pop()
        u = found[0] + found[1] + found[2]
        if k + 1 < TRI_CHUNKS:
            ahead.append(find(k + 1))

        def factor(j, m):
            return factors[pl.ds(pl.multiple_of((9 * j + m) * TRI_ROWS + k * GROUPS, GROUPS), GROUPS), :]

        inner = [sum(factor(j, m) * u[j] for j in range(9)) * (1.0 / 9.0) for m in range(9)]
        shift = REG * valid_of(whole, k)
        out = [sum(factor(j, m) * inner[m] for m in range(9)) + shift * u[j] for j in range(9)]
        spread_out([out[0:3], out[3:6], out[6:9]], k, hot_row, stage.at[turn], spread)

    sweep(build, hot_lane, spreads, total)


def inertia_of(whole):
    return [lane_rows(whole, INERTIA + k) for k in range(VERT_CHUNKS)]


def apply_local(whole, factors, hots, field, words, stage, spreads, total, befores=None, afters=None):
    elements(whole, factors, *hots, field, words, stage, spreads, total)
    mass = inertia_of(whole)
    out = []
    for c in range(3):
        v = chunks(field, c)
        bent = chain(v, befores and befores[c], afters and afters[c])
        felt = chunks(total, c)
        out.append([mass[k] * v[k] + bent[k] + felt[k] for k in range(VERT_CHUNKS)])
    return out


def setup_kernel(whole, weights, factors, hot_lane, hot_row, first, image, diagonal, up, down,
                 pos, feats, inputs, outputs, raw, stage6, spread6a, spread6b, total6,
                 words, stage, spread_a, spread_b, total):
    for c in range(3):
        put(pos, c, [lane_rows(whole, POS + 3 * k + c) for k in range(VERT_CHUNKS)])
    feats[...] = jnp.zeros_like(feats)

    for k in range(TRI_CHUNKS):
        feat = feats.at[k % 2]
        places = [corner_of(whole, k, q) for q in range(3)]
        for q, (row, lane) in enumerate(places):
            one_hot(row, lane, q, k, hot_lane, hot_row, stage.at[k % 2, q])
        x0, x1, x2 = gather(pos, places)
        a, b, c_, d = [lane_rows(whole, RINV + 4 * k + i) for i in range(4)]
        for c in range(3):
            one, two = x1[c] - x0[c], x2[c] - x0[c]
            feat[pl.ds(c, GROUPS, stride=16), :] = one * a + two * c_
            feat[pl.ds(3 + c, GROUPS, stride=16), :] = one * b + two * d
        inputs[k] = jnp.concatenate([feat[16 * e : 16 * e + 16, :] for e in range(GROUPS)], axis=1).astype(BF16)

    x = jnp.concatenate([inputs[k] for k in range(TRI_CHUNKS)], axis=1)
    h = lax.dot_general(weights[0:HID1], x, (((0,), (0,)), ((), ())), preferred_element_type=F32)
    h = jnp.tanh(h).astype(BF16)
    for weight in (weights[HID1:HID2], weights[HID2:LAST]):
        h = jnp.tanh(jnp.dot(weight, h, preferred_element_type=F32)).astype(BF16)
    o = jnp.dot(weights[LAST:WEIGHTS], h, preferred_element_type=F32)
    for k in range(TRI_CHUNKS):
        outputs[k] = o[:, k * GROUPS * LANES : (k + 1) * GROUPS * LANES]

    def build(k, spread, turn):
        for e in range(GROUPS):
            for g in range(12):
                raw[pl.ds(g * 64 + e, 8, stride=8), :] = outputs[k, 8 * g : 8 * g + 8, e * LANES : (e + 1) * LANES]
        valid = valid_of(whole, k)
        forces, curves = [], []
        for j in range(9):
            forces.append(raw[8 * j : 8 * j + 8, :] * valid)
            curve = 0.0
            for m in range(9):
                at = 9 * j + m
                g = (raw[8 * (9 + at) : 8 * (9 + at) + 8, :] * valid).astype(BF16).astype(F32)
                factors[pl.ds(pl.multiple_of(at * TRI_ROWS + k * GROUPS, GROUPS), GROUPS), :] = g
                curve += g * g
            curves.append(curve * (1.0 / 9.0) + REG * valid)
        values = [forces[3 * q : 3 * q + 3] + curves[3 * q : 3 * q + 3] for q in range(3)]
        spread_out(values, k, hot_row, stage6.at[turn], spread)

    sweep(build, hot_lane, (spread6a, spread6b), total6)
    mass = inertia_of(whole)
    inverse = []
    for c in range(3):
        x = chunks(pos, c)
        bent = chain(x, whole[(GROUPS - 1) * PACKED + RIM + c : (GROUPS - 1) * PACKED + RIM + c + 1, :],
                     whole[RIM + c : RIM + c + 1, :])
        felt, curve = chunks(total6, c), chunks(total6, 3 + c)
        diag = [mass[k] + curve[k] + 2.0 * STIFF for k in range(VERT_CHUNKS)]
        inv = [1.0 / diag[k] for k in range(VERT_CHUNKS)]
        grad = [mass[k] * (x[k] - lane_rows(whole, TGT + 3 * k + c)) + bent[k] + felt[k]
                for k in range(VERT_CHUNKS)]
        put(diagonal, c, diag)
        put(first, c, [-grad[k] * inv[k] for k in range(VERT_CHUNKS)])
        inverse.append(inv)
    w = apply_local(whole, factors, (hot_lane, hot_row), first, words, stage, (spread_a, spread_b), total)
    up[...] = jnp.zeros_like(up)
    down[...] = jnp.zeros_like(down)
    for c in range(3):
        v = chunks(first, c)
        put(image, c, w[c])
        nxt = [w[c][k] * inverse[c][k] - v[k] for k in range(VERT_CHUNKS)]
        for i, what in enumerate((v, nxt, inverse[c])):
            up[3 * i + c : 3 * i + c + 1, :] = what[1][GROUPS - 1 : GROUPS, :]
            down[3 * i + c : 3 * i + c + 1, :] = what[0][0:1, :]


def krylov_kernel(whole, factors, hot_lane, hot_row, first, image, diagonal, above, below,
                  second, third, last_image, sums, words, stage, spread_a, spread_b, total):
    hots, spreads = (hot_lane, hot_row), (spread_a, spread_b)
    lane = iota((GROUPS, LANES), 1)
    sub = iota((GROUPS, LANES), 0)
    head = (lane == 0) & (sub == 0)
    tail = (lane == LANES - 1) & (sub == GROUPS - 1)

    def spread(row):
        return jnp.broadcast_to(row, (GROUPS, LANES))

    befores, afters = [], []
    for c in range(3):
        v0, w0 = chunks(first, c), chunks(image, c)
        diag = chunks(diagonal, c)
        inv = [1.0 / diag[k] for k in range(VERT_CHUNKS)]
        old_up, old_down = above[c : c + 1, :], below[c : c + 1, :]
        w_low = w0[0] - STIFF * jnp.where(head, pltpu.roll(spread(old_up), 1, 1), 0.0)
        w_high = w0[1] - STIFF * jnp.where(tail, pltpu.roll(spread(old_down), LANES - 1, 1), 0.0)
        put(second, c, [w_low * inv[0] - v0[0], w_high * inv[1] - v0[1]])
        mine_low = pltpu.roll(spread(v0[0][0:1, :]), LANES - 1, 1)[0:1, :]
        mine_high = pltpu.roll(spread(v0[1][GROUPS - 1 : GROUPS, :]), 1, 1)[0:1, :]
        befores.append(above[3 + c : 4 + c, :] - STIFF * mine_low * above[6 + c : 7 + c, :])
        afters.append(below[3 + c : 4 + c, :] - STIFF * mine_high * below[6 + c : 7 + c, :])
    w = apply_local(whole, factors, hots, second, words, stage, spreads, total, befores, afters)
    for c in range(3):
        diag, v1 = chunks(diagonal, c), chunks(second, c)
        put(third, c, [w[c][k] / diag[k] - v1[k] for k in range(VERT_CHUNKS)])
    w = apply_local(whole, factors, hots, third, words, stage, spreads, total)
    moment = [0.0] * 6
    ends = []
    for c in range(3):
        put(last_image, c, w[c])
        diag = chunks(diagonal, c)
        v0, v1, v2 = chunks(first, c), chunks(second, c), chunks(third, c)
        for k in range(VERT_CHUNKS):
            m0, m1, m2 = diag[k] * v0[k], diag[k] * v1[k], diag[k] * v2[k]
            for i, term in enumerate((m0 * v0[k], m0 * v1[k], m1 * v1[k], m1 * v2[k], m2 * v2[k],
                                      v2[k] * w[c][k] - m2 * v2[k])):
                moment[i] += term
        ends.append((jnp.where(head, v2[0], 0.0), jnp.where(tail, v2[1], 0.0)))
    line = jnp.zeros((1, LANES), F32)
    for i, part in enumerate(moment + [x[0] for x in ends] + [x[1] for x in ends]):
        value = jnp.sum(jnp.sum(part, axis=0, keepdims=True), axis=1, keepdims=True)
        line = jnp.where(iota((1, LANES), 1) == i, value, line)
    sums[...] = jnp.broadcast_to(line[:, 0:SHARED], sums.shape)


def finish_kernel(sums, first, second, third, last_image, diagonal, field, residual):
    patch, elem = lax.axis_index("patch"), lax.axis_index("elem")
    patches = sums.shape[0]
    every = sums[...]
    lane = iota(every.shape, 1)
    sub = iota(every.shape, 0)
    totals = jnp.sum(every, axis=0, keepdims=True)

    def pick(row, i):
        return row[:, i : i + 1]

    after = pltpu.roll(pltpu.roll(every, patches - 1, 0), 3, 1)
    coupled = jnp.where((lane >= 9) & (lane < 12) & (sub < patches - 1), every * after, 0.0)
    coupling = jnp.sum(jnp.sum(coupled, axis=0, keepdims=True), axis=1, keepdims=True)
    mu = [pick(totals, i) for i in range(6)]
    mu[5] = mu[5] - 2.0 * STIFF * coupling

    def inner(p, q):
        return sum(a * b * mu[i + j] for i, a in enumerate(p) for j, b in enumerate(q))

    def applied(p):
        padded = list(p) + [0.0 * mu[0]]
        return [padded[0]] + [padded[j] + padded[j - 1] for j in range(1, len(padded))]

    one = jnp.ones((1, 1), F32)
    z, direction, x = [one], [one], []
    rz = inner(z, z)
    for step in range(3):
        ahead = applied(direction)
        alpha = rz / inner(direction, ahead)
        x = [(x[j] if j < len(x) else 0.0) + alpha * direction[j] for j in range(len(direction))]
        z = [(z[j] if j < len(z) else 0.0) - alpha * ahead[j] for j in range(len(ahead))]
        if step < 2:
            new = inner(z, z)
            ratio = new / rz
            direction = [z[j] + (ratio * direction[j] if j < len(direction) else 0.0) for j in range(len(z))]
            rz = new
    place = iota((1, LANES), 1)
    prev = sums[pl.ds(jnp.maximum(patch - 1, 0), 1), :]
    nxt = sums[pl.ds(jnp.minimum(patch + 1, patches - 1), 1), :]
    at_head = (place == 0) & (elem == 0) & (patch > 0)
    at_tail = (place == LANES - 1) & (elem == GROUPS - 1) & (patch < patches - 1)
    for c in range(3):
        for k in range(VERT_CHUNKS):
            at = pl.ds(c * ROWS + k * GROUPS + elem, 1)
            v0, v1, v2, w2, diag = first[at, :], second[at, :], third[at, :], last_image[at, :], diagonal[at, :]
            if k == 0:
                w2 = w2 - STIFF * jnp.where(at_head, pick(prev, 9 + c), 0.0)
            else:
                w2 = w2 - STIFF * jnp.where(at_tail, pick(nxt, 6 + c), 0.0)
            v3 = w2 / diag - v2
            cut = slice(k * LANES, (k + 1) * LANES)
            field[c : c + 1, cut] = x[0] * v0 + x[1] * v1 + x[2] * v2
            residual[c : c + 1, cut] = diag * (z[0] * v0 + z[1] * v1 + z[2] * v2 + z[3] * v3)


def shape(*dims):
    return jax.ShapeDtypeStruct(dims, F32)


def per_device(positions, target, inertia, incidence, rest_inverse, counts, w_in, w_hid1, w_hid2, w_out):
    patches = lax.axis_size("patch")
    params = pltpu.CompilerParams(vmem_limit_bytes=20 * 1024 * 1024)
    moves = []
    for p in range(patches - 1):
        left, right = p * GROUPS, (p + 1) * GROUPS
        moves += [(left + GROUPS - 1, right + GROUPS - 1), (right, left)]
    rim = lax.ppermute(positions, ("patch", "elem"), moves)
    packed, weights = pl.pallas_call(
        pack_kernel, out_shape=[shape(GROUPS, PACKED, LANES), jax.ShapeDtypeStruct((WEIGHTS, LANES), BF16)],
        in_specs=vmem(9), out_specs=vmem(2), name="pack",
    )(positions, target, inertia, incidence, rest_inverse, w_in.T, w_hid1, w_hid2, w_out)
    packed, weights = pl.pallas_call(
        rim_kernel, grid=(1,),
        out_shape=[shape(GROUPS, PACKED, LANES), jax.ShapeDtypeStruct(weights.shape, weights.dtype)],
        in_specs=[pl.BlockSpec(memory_space=pl.ANY)] + vmem(1) + [pl.BlockSpec(memory_space=pltpu.SMEM)]
        + [pl.BlockSpec(memory_space=pl.ANY)],
        out_specs=[pl.BlockSpec((GROUPS, PACKED - RIM, LANES), lambda i: (0, RIM // (PACKED - RIM), 0)),
                   pl.BlockSpec(memory_space=pl.ANY)],
        input_output_aliases={0: 0, 3: 1}, compiler_params=params, name="rim",
    )(packed, rim, counts, weights)
    whole = lax.all_to_all(packed, "elem", 0, 0, tiled=True).reshape(GROUPS * PACKED, LANES)
    wide = 3 * ROWS
    width = GROUPS * LANES
    words = [pltpu.VMEM((2 * ROWS, LANES), jnp.int32)]

    def scatter_scratch(comps):
        spread = pltpu.VMEM((2 * comps * ROWS, 3 * width), BF16)
        return [pltpu.VMEM((2, 3, 2 * comps * GROUPS, LANES), F32), spread, spread,
                pltpu.VMEM((2 * comps * ROWS, LANES), F32)]

    factors, hot_lane, hot_row, first, image, diagonal, up, down = pl.pallas_call(
        setup_kernel,
        out_shape=[shape(81 * TRI_ROWS, LANES), jax.ShapeDtypeStruct((TRI_CHUNKS, LANES, 3 * width), BF16),
                   jax.ShapeDtypeStruct((TRI_CHUNKS, ROWS, 3 * width), BF16),
                   shape(wide, LANES), shape(wide, LANES), shape(wide, LANES), shape(16, LANES), shape(16, LANES)],
        in_specs=vmem(2), out_specs=vmem(8),
        scratch_shapes=[pltpu.VMEM((wide, LANES), F32), pltpu.VMEM((2, GROUPS * 16, LANES), F32),
                        pltpu.VMEM((TRI_CHUNKS, 16, width), BF16), pltpu.VMEM((TRI_CHUNKS, 96, width), F32),
                        pltpu.VMEM((96 * GROUPS, LANES), F32)] + scatter_scratch(6) + words + scatter_scratch(3),
        compiler_params=params, name="setup",
    )(whole, weights)
    above = lax.ppermute(up, "patch", [(p, p + 1) for p in range(patches - 1)])
    below = lax.ppermute(down, "patch", [(p + 1, p) for p in range(patches - 1)])
    second, third, last_image, sums = pl.pallas_call(
        krylov_kernel,
        out_shape=[shape(wide, LANES), shape(wide, LANES), shape(wide, LANES), shape(patches, SHARED)],
        in_specs=vmem(9), out_specs=vmem(4), scratch_shapes=words + scatter_scratch(3),
        compiler_params=params, name="krylov",
    )(whole, factors, hot_lane, hot_row, first, image, diagonal, above, below)
    sums = lax.all_to_all(sums, "patch", 0, 0, tiled=True)
    return pl.pallas_call(
        finish_kernel, out_shape=[shape(*positions.shape)] * 2,
        in_specs=vmem(6), out_specs=vmem(2), compiler_params=params, name="finish",
    )(sums, first, second, third, last_image, diagonal)


def solution(mesh):
    split = P(None, ("patch", "elem"))
    placed = (split,) * 5 + (P(("patch", "elem")),) + (P(),) * 4
    return jax.shard_map(per_device, mesh=mesh, in_specs=placed, out_specs=(split, split), check_vma=False)
```
